256 devices in a mesh: sec: 2 (over core), row: 8 (over y, z_lo), col: 16 (over z_hi, x).
Axes of the slice: x: 4, y: 4, z: 8 (z_hi: 4, z_lo: 2; z = z_hi * 2 + z_lo), core: 2. Of those that a mesh axis runs over, the one named last changes fastest.
Arguments:
- anc_inverse: float32 [4096, 4096], P('row', ('sec', 'col')), as said below
- panel: float32 [32768, 4096], P(('sec', 'col'), 'row'), may hold values from -0.375 to 0.375
- diag_inverse: float32 [32768, 512], P(('sec', 'col')), may hold values from -6 to 6
- widths: int32 [64], replicated, may hold values from 1 to 4, as said below
- pattern: int32 [64, 32], replicated, may hold values 0 or 1
Outputs:
- off_inverse: float32 [32768, 4096], P(('sec', 'col'), 'row')
- child_inverse: float32 [32768, 512], P(('sec', 'col'))
The draws below stay inside these ranges and needn't reach their ends.
Inputs may be any that keep to these rules, and one draw needn't show every extreme that they name: `anc_inverse`: exactly symmetric. `widths`: both 1 and 4 occur in every draw.
All inputs are finite; a program needn't handle non-finite values.
Results may differ from the reference program's by a relative error of at most 0.0003.
Values sent between devices are 32-bit elements; how exact they have to be, the bound alone decides.
No kernel may reach another device: no remote copies, remote signals or barrier semaphores. Data moves between devices by JAX's collectives and lax.ppermute only.
A program may use at most 128 MiB of HBM per device.

```python
import math
import jax
import jax.numpy as jnp
from jax import lax

B = 128
WMAX = 4
SW = 512
NA = 4096
NAB = 32
SLOTS = 64
CHILD_COLS = 32768


def draw_anc_inverse(key, part):
    first_key, second_key = jax.random.split(jax.random.fold_in(key, 11), 2)
    rough = jax.random.normal(first_key, (NA, NA), jnp.float32)
    symmetric = (rough + rough.T) * (0.5 ** 0.5 / math.sqrt(NA))
    diagonal = jnp.exp(jax.random.uniform(second_key, (NA,), jnp.float32, 0.0, math.log(4.0)))
    return symmetric + jnp.diag(diagonal)


def draw_widths(key, part):
    first_key, second_key = jax.random.split(jax.random.fold_in(key, 23))
    drawn = jax.random.randint(first_key, (SLOTS,), 1, WMAX + 1)
    spots = jax.random.permutation(second_key, SLOTS)
    drawn = drawn.at[spots[0]].set(WMAX).at[spots[1]].set(1)
    return drawn.astype(jnp.int32)


def touch_ends(entries, own_key, smallest, largest):
    place = [jax.random.randint(jax.random.fold_in(own_key, axis), (), 0, length) for axis, length in enumerate(entries.shape)]
    longest = entries.shape.index(max(entries.shape))
    neighbour = place[:longest] + [(place[longest] + 1) % entries.shape[longest]] + place[longest + 1:]
    return entries.at[tuple(place)].set(smallest).at[tuple(neighbour)].set(largest)


def levels(key, extent, cuts, low, largest):
    level = 1.0
    for axis_at, blocks in cuts:
        draws = jax.random.uniform(jax.random.fold_in(jax.random.fold_in(key, 6), axis_at), (blocks,), jnp.float32, low / len(cuts), largest / len(cuts))
        level = level * jnp.repeat(jnp.exp(draws), extent[axis_at] // blocks).reshape((-1,) + (1,) * (len(extent) - 1 - axis_at))
    return level


def gaussian(rng, shape, deviation, most, shards=(), kind=jnp.bfloat16):
    result = jax.random.normal(rng, shape, jnp.float32) * deviation
    if len(shards) > 0:
        result = levels(rng, shape, shards, -0.22, 0.18) * result
    return jnp.clip(result, min=-most, max=most).astype(kind)


def setup_inputs(seed: int = 0) -> dict:
    key_list = jax.random.split(jax.random.key(seed), 6)
    return {
        "anc_inverse": draw_anc_inverse(jax.random.fold_in(key_list[5], 71), 0),
        "panel": gaussian(key_list[1], (CHILD_COLS, NA), (NA // 16) ** -0.5, 0.375, ((0, 32), (1, 8)), jnp.float32),
        "diag_inverse": gaussian(key_list[2], (CHILD_COLS, SW), 1.0, 6.0, ((0, 32),), jnp.float32),
        "widths": draw_widths(jax.random.fold_in(key_list[5], 71), 0),
        "pattern": touch_ends((jax.random.randint(key_list[4], (SLOTS, NAB), 0, 2) < 1).astype(jnp.int32), jax.random.fold_in(key_list[4], 1), 0, 1),
    }


def reference(anc_inverse, panel, diag_inverse, widths, pattern):
    highest = lax.Precision.HIGHEST
    position = jnp.arange(SW, dtype=jnp.int32)

    def solve_slot(inputs):
        slot_panel, slot_diag, slot_blocks, slot_pattern = inputs
        column_mask = (position < slot_blocks * B).astype(jnp.float32)
        row_mask = jnp.repeat(slot_pattern.astype(jnp.float32), B)
        masked = slot_panel * column_mask[:, None] * row_mask[None, :]
        product = jnp.dot(masked, anc_inverse, precision=highest, preferred_element_type=jnp.float32)
        product = product * column_mask[:, None] * row_mask[None, :]
        update = jnp.dot(product, masked.T, precision=highest, preferred_element_type=jnp.float32)
        diag_block = (slot_diag + update) * column_mask[:, None] * column_mask[None, :]
        return -product, diag_block

    off_blocks, diag_blocks = lax.map(
        solve_slot,
        (panel.reshape(SLOTS, SW, NA), diag_inverse.reshape(SLOTS, SW, SW), widths, pattern),
    )
    return off_blocks.reshape(SLOTS * SW, NA), diag_blocks.reshape(SLOTS * SW, SW)
```

```python
import jax
import jax.numpy as jnp
import numpy as np
from jax import lax
from jax.sharding import Mesh, PartitionSpec as P

B = 128
SW = 512
HIGH = lax.Precision.HIGH
ROW = ("y", "zl")
Z = ("zl", "zh")
CHUNK = 256


def z_rounds():
    even = [
        {0: 0, 2: 1, 4: 4, 6: 5},
        {6: 0, 0: 1, 2: 4, 4: 5},
        {2: 0, 4: 1, 6: 4, 0: 5},
        {4: 0, 6: 1, 0: 4, 2: 5},
    ]
    rounds = []
    table = np.zeros((8, 2, 2), np.int32)
    for k, pairs in enumerate(even):
        pairs = {**pairs, **{(3 - t) % 8: (3 - s) % 8 for t, s in pairs.items()}}
        rounds.append([((s % 2) * 4 + s // 2, (t % 2) * 4 + t // 2) for t, s in pairs.items()])
        for t, s in pairs.items():
            table[t, int(s % 2 == t % 2), (s // 2) // 2] = k
    return rounds, table


def step(value, axis, k, n=4):
    return lax.ppermute(value, axis, [(i, (i + k) % n) for i in range(n)])


def local(anc_inverse, panel, diag_inverse, widths, pattern):
    core, y, zl = lax.axis_index("core"), lax.axis_index("y"), lax.axis_index("zl")
    zh, x = lax.axis_index("zh"), lax.axis_index("x")
    chunks = panel.shape[0] // CHUNK
    parts = [panel[i * CHUNK : (i + 1) * CHUNK] for i in range(chunks)]
    half = CHUNK // 2

    direct, relay = [None] * chunks, [None] * chunks

    def send_direct(i):
        direct[i] = (step(parts[i], "y", 1), step(parts[i], "y", -1))

    def send_relay(i):
        left, right = direct[i]
        relay[i] = (step(left[:half], "y", 1), step(right[half:], "y", -1))

    send_direct(0)
    rounds, table = z_rounds()
    got = jnp.stack([lax.ppermute(anc_inverse, Z, pairs) for pairs in rounds])
    send_direct(1)
    for i in range(2, chunks):
        parts[i], direct[i - 2] = lax.optimization_barrier((parts[i], direct[i - 2]))
        send_relay(i - 2)
        send_direct(i)
    send_relay(chunks - 2)
    send_relay(chunks - 1)

    places = jnp.asarray(table)[zh * 2 + zl]
    order = [(y + d) % 4 for d in (0, 3, 1, 2)]

    def gather(role):
        piece = jnp.stack(
            [lax.dynamic_index_in_dim(got, places[role, k], 0, keepdims=False) for k in range(2)]
        )
        left, right = step(piece, "x", 1), step(piece, "x", -1)
        far = jnp.stack([step(left[0], "x", 1), step(right[1], "x", -1)])
        mine = jnp.zeros((2, 4) + piece.shape[1:], jnp.float32)
        for value, d in ((piece, 0), (left, 3), (right, 1), (far, 2)):
            mine = lax.dynamic_update_slice_in_dim(mine, value[:, None], (x + d) % 4, 1)
        theirs = step(mine, "core", 1, 2)
        whole = jnp.zeros((2,) + mine.shape, jnp.float32)
        whole = lax.dynamic_update_index_in_dim(whole, mine, core, 0)
        whole = lax.dynamic_update_index_in_dim(whole, theirs, 1 - core, 0)
        whole = whole.reshape((4,) + mine.shape[1:])
        blocks = [lax.dynamic_index_in_dim(whole, o, 0, keepdims=False) for o in order]
        blocks = [b.transpose(1, 0, 2).reshape(b.shape[1], 4 * B) for b in blocks]
        return jnp.concatenate(blocks, axis=1)

    anc_other = gather(0)
    anc_own = gather(1)

    slots = panel.shape[0] // SW
    first = ((core * 4 + zh) * 4 + x) * slots
    my_widths = lax.dynamic_slice_in_dim(widths, first, slots)
    my_pattern = lax.dynamic_slice_in_dim(pattern, first, slots, 0).astype(jnp.float32)
    position = jnp.arange(SW, dtype=jnp.int32)
    column_mask = (position[None, :] < my_widths[:, None] * B).astype(jnp.float32)
    by_row = my_pattern.reshape(slots, 4, 2, 4)
    by_row = lax.dynamic_index_in_dim(by_row, zl, 2, keepdims=False)
    by_row = jnp.concatenate([lax.dynamic_slice_in_dim(by_row, o, 1, 1) for o in order], axis=1)
    row_mask = jnp.repeat(by_row.reshape(slots, 16), B, axis=1)

    def dot(a, b):
        return lax.dot_general(
            a, b, (((1,), (1,)), ((), ())), precision=HIGH, preferred_element_type=jnp.float32
        )

    per = SW // CHUNK
    off, updates = [], []
    for i in range(chunks):
        child = i // per
        rows = column_mask[child, (i % per) * CHUNK : (i % per + 1) * CHUNK]
        far = jnp.concatenate(relay[i], axis=0)
        full = jnp.concatenate([parts[i], *direct[i], far], axis=1)
        full = full * rows[:, None] * row_mask[child][None, :]
        received = step(dot(full, anc_other), "zl", 1, 2)
        product = dot(full, anc_own) + received
        product = product * rows[:, None] * row_mask[child][None, :SW]
        off.append(-product)
        own = panel[child * SW : (child + 1) * SW]
        own = own * column_mask[child][:, None] * row_mask[child][None, :SW]
        updates.append(dot(product, own))

    blocks = []
    for child in range(slots):
        update = jnp.concatenate(updates[child * per : (child + 1) * per], axis=0)
        for a in range(4):
            for b in range(a + 1):
                blocks.append(update[a * B : (a + 1) * B, b * B : (b + 1) * B])
    packed = jnp.concatenate(blocks, axis=0)
    packed = packed.reshape(8, packed.shape[0] // 8, B)
    mine = lax.all_to_all(packed, ROW, 0, 0, tiled=True).sum(0)
    summed = lax.all_to_all(jnp.broadcast_to(mine, packed.shape), ROW, 0, 0, tiled=True)
    summed = summed.reshape(-1, B, B)
    children = []
    for child in range(slots):
        rows = []
        for a in range(4):
            row = []
            for b in range(4):
                low, high = min(a, b), max(a, b)
                block = summed[child * 10 + high * (high + 1) // 2 + low]
                row.append(block if a >= b else block.T)
            rows.append(jnp.concatenate(row, axis=1))
        value = jnp.concatenate(rows, axis=0) + diag_inverse[child * SW : (child + 1) * SW]
        children.append(value * column_mask[child][:, None] * column_mask[child][None, :])
    return jnp.concatenate(off, axis=0), jnp.concatenate(children, axis=0)


def solution(mesh):
    fine = Mesh(mesh.devices.reshape(2, 4, 2, 4, 4), ("core", "y", "zl", "zh", "x"))
    group = ("core", "zh", "x")
    in_specs = (P(ROW, group), P(group, ROW), P(group, None), P(), P())
    out_specs = (P(group, ROW), P(group, None))
    return jax.shard_map(local, mesh=fine, in_specs=in_specs, out_specs=out_specs, check_vma=False)
```

```python
import functools

import jax
import jax.numpy as jnp
from jax import lax
from jax.experimental import pallas as pl
from jax.experimental.pallas import tpu as pltpu
from jax.sharding import Mesh, PartitionSpec as P

B = 128
SW = 512
WIDE = 2048
LIMIT = 18 * 2**20
ROW = ("y", "zl")
Z = ("zl", "zh")
DIRECTIONS = (0, 3, 1, 2)

VMEM = pl.BlockSpec(memory_space=pltpu.VMEM)
SMEM = pl.BlockSpec(memory_space=pltpu.SMEM)
F32 = jnp.float32
BF16 = jnp.bfloat16


def call(kernel, out_shape, specs, out_specs=None, scratch=(), aliases=None):
    single = not isinstance(out_shape, (tuple, list))
    return pl.pallas_call(
        kernel,
        out_shape=out_shape,
        in_specs=specs,
        out_specs=out_specs if out_specs is not None else (VMEM if single else [VMEM] * len(out_shape)),
        scratch_shapes=list(scratch),
        input_output_aliases=aliases or {},
        compiler_params=pltpu.CompilerParams(vmem_limit_bytes=LIMIT),
        cost_estimate=pl.CostEstimate(flops=1024, bytes_accessed=1024, transcendentals=0),
    )


def struct(shape, dtype=F32):
    return jax.ShapeDtypeStruct(shape, dtype)


def z_rounds():
    even = [
        {0: 0, 2: 1, 4: 4, 6: 5},
        {6: 0, 0: 1, 2: 4, 4: 5},
        {2: 0, 4: 1, 6: 4, 0: 5},
        {4: 0, 6: 1, 0: 4, 2: 5},
    ]
    rounds = []
    table = {}
    for k, pairs in enumerate(even):
        pairs = {**pairs, **{(3 - t) % 8: (3 - s) % 8 for t, s in pairs.items()}}
        rounds.append([((s % 2) * 4 + s // 2, (t % 2) * 4 + t // 2) for t, s in pairs.items()])
        for t, s in pairs.items():
            table[t, int(s % 2 == t % 2), (s // 2) // 2] = k
    return rounds, table


def step(value, axis, k, n=4):
    return lax.ppermute(value, axis, [(i, (i + k) % n) for i in range(n)])


def split(value):
    high = value.astype(BF16)
    return high, (value - high.astype(F32)).astype(BF16)


def dot3(a, b):
    dims = (((1,), (1,)), ((), ()))
    mul = functools.partial(lax.dot_general, dimension_numbers=dims, preferred_element_type=F32)
    return mul(a[0], b[0]) + (mul(a[0], b[1]) + mul(a[1], b[0]))


def meta_kernel(ids, widths, pattern, out):
    core, y, zl, zh, x = (ids[i] for i in range(5))
    first = ((core * 4 + zh) * 4 + x) * 2
    for child in range(2):
        for d, shift in enumerate(DIRECTIONS):
            block = ((y + shift) % 4 * 2 + zl) * 4
            for k in range(4):
                value = pattern[first + child, block + k].astype(F32)
                out[child : child + 1, (d * 4 + k) * B : (d * 4 + k + 1) * B] = jnp.full((1, B), value)
        out[2 + child : 3 + child, :] = jnp.full((1, WIDE), (widths[first + child] * B).astype(F32))
        block = (y * 2 + 1 - zl) * 4
        for k in range(4):
            value = pattern[first + child, block + k].astype(F32)
            out[4 + child : 5 + child, k * B : (k + 1) * B] = jnp.full((1, B), value)
        out[4 + child : 5 + child, SW:] = jnp.zeros((1, WIDE - SW), F32)
    out[6:8, :] = jnp.zeros((2, WIDE), F32)


def column_mask(meta, child):
    position = lax.broadcasted_iota(jnp.int32, (SW, B), 0).astype(F32)
    return (position < meta[2 + child : 3 + child, :B]).astype(F32)


def select_kernel(table, ids, r0, r1, r2, r3, other, own):
    z = ids[3] * 2 + ids[2]
    for role, out in enumerate((other, own)):
        for k in range(2):
            place = jnp.int32(0)
            for at in range(8):
                place = jnp.where(z == at, table[at, role, k], place)
            for i, source in enumerate((r0, r1, r2, r3)):

                @pl.when(place == i)
                def _():
                    out[k] = source[...]


def join_kernel(piece, left, right, top, bottom, out):
    out[0], out[1], out[2] = piece[...], left[...], right[...]
    out[3, 0], out[3, 1] = top[...], bottom[...]


def prepare_kernel(ids, mine, theirs, high, low):
    core, y, x = ids[0], ids[1], ids[4]
    for d, shift in enumerate(DIRECTIONS):
        block = (y + shift) % 4
        here = block // 2 == core
        for k in range(4):
            away = (k - x + 4) % 4
            at = jnp.where(away == 0, 0, jnp.where(away == 3, 1, jnp.where(away == 1, 2, 3)))
            columns = slice((d * 4 + k) * B, (d * 4 + k + 1) * B)

            def put(source):
                high[:, columns], low[:, columns] = split(source[at, block % 2])

            pl.when(here)(lambda: put(mine))
            pl.when(jnp.logical_not(here))(lambda: put(theirs))


def product_kernel(child, own, left, right, top, bottom, high, low, meta, out, phigh, plow):
    rows = own.shape[0]
    half = rows // 2
    mask = column_mask(meta, child)
    for d, source in enumerate((own, left, right, None)):
        for k in range(4):
            at = (d * 4 + k) * B
            lanes = slice(at, at + B)
            here = slice(k * B, (k + 1) * B)
            if source is None:
                parts = ((top, 0, half), (bottom, half, rows))
            else:
                parts = ((source, 0, rows),)
            for ref, low_row, high_row in parts:
                value = ref[:, here] * mask[low_row:high_row] * meta[child : child + 1, lanes]
                phigh[low_row:high_row, lanes], plow[low_row:high_row, lanes] = split(value)
    for n in range(0, 512, 256):
        b = (high[n : n + 256, :], low[n : n + 256, :])
        for r in range(0, rows, 256):
            out[r : r + 256, n : n + 256] = dot3((phigh[r : r + 256, :], plow[r : r + 256, :]), b)


def lower_blocks(update, pairs):
    at = 0
    for a in range(4):
        value = None
        for left, right in pairs:
            term = dot3([v[a * B : (a + 1) * B] for v in left], [v[: (a + 1) * B] for v in right])
            value = term if value is None else value + term
        for b in range(a + 1):
            update[at * B : (at + 1) * B, :] = value[:, b * B : (b + 1) * B]
            at += 1


def masked(child, panel, meta, row):
    wide = jnp.concatenate([column_mask(meta, child)] * 4, axis=1)
    return panel[...] * wide * meta[row : row + 1, :SW]


def finish_kernel(child, mine, received, panel, meta, *refs):
    wide = jnp.concatenate([column_mask(meta, child)] * 4, axis=1)
    product = (mine[...] + received[...]) * wide * meta[child : child + 1, :SW]
    if child == 0:
        off, update = refs
        lower_blocks(update, [(split(product), split(masked(child, panel, meta, child)))])
    else:
        off = refs[-1]
    off[...] = -product


def update_kernel(child, mine, theirs, panel, across, meta, update):
    lower_blocks(
        update,
        [
            (split(mine[...]), split(masked(child, panel, meta, child))),
            (split(theirs[...]), split(masked(child, across, meta, 4 + child))),
        ],
    )


def sum_kernel(parts, out):
    total = parts[0]
    for k in range(1, 8):
        total += parts[k]
    for k in range(8):
        out[k] = total


def child_kernel(parts, diag, meta, out):
    at = 0
    for child in range(2):
        across = lax.broadcasted_iota(jnp.int32, (1, SW), 1).astype(F32) < meta[2 + child : 3 + child, :SW]
        across = across.astype(F32)
        mask = column_mask(meta, child)
        for a in range(4):
            for b in range(a + 1):
                block = parts[at]
                at += 1
                for (i, j), value in {(b, a): block.T, (a, b): block}.items():
                    lines = slice(child * SW + i * B, child * SW + (i + 1) * B)
                    lanes = slice(j * B, (j + 1) * B)
                    rows = mask[i * B : (i + 1) * B]
                    out[lines, lanes] = (diag[lines, lanes] + value) * rows * across[:, lanes]


def after(value, *before):
    if not before:
        return value
    return lax.optimization_barrier((value, *before))[0]


def local(anc_inverse, panel, diag_inverse, widths, pattern):
    names = ("core", "y", "zl", "zh", "x")
    ids = jnp.stack([lax.axis_index(n) for n in names]).astype(jnp.int32)
    parts = [panel[:SW], panel[SW:]]

    def send_direct(i):
        return step(parts[i], "y", 1), step(parts[i], "y", -1)

    def send_relay(left, right):
        half = SW // 2
        return step(left[:half], "y", 1), step(right[half:], "y", -1)

    rounds, table = z_rounds()
    direct = [send_direct(0)]
    got = [lax.ppermute(anc_inverse, Z, pairs) for pairs in rounds]
    direct.append(send_direct(1))
    across = step(parts[1], "zl", 1, 2)
    relay = [send_relay(*direct[0]), send_relay(*direct[1])]

    got[0] = after(got[0], *direct[0])
    piece = struct((2, 512, B))
    pieces = call(functools.partial(select_kernel, table), (piece, piece), [SMEM] + [VMEM] * 4)(ids, *got)
    meta = call(meta_kernel, struct((8, WIDE)), [SMEM] * 3)(ids, widths, pattern)

    def gather(value, before, far, joined, swapped):
        value = after(value, *before)
        left, right = step(value, "x", 1), step(value, "x", -1)
        top, bottom = step(after(left[0], *far), "x", 1), step(after(right[1], *far), "x", -1)
        top = after(top, *joined)
        mine = call(join_kernel, struct((4, 2, 512, B)), [VMEM] * 5)(value, left, right, top, bottom)
        theirs = after(step(mine, "core", 1, 2), *swapped)
        pair = struct((512, WIDE), BF16)
        return call(prepare_kernel, (pair, pair), [SMEM, VMEM, VMEM])(ids, mine, theirs), (left, right)

    other, before = gather(pieces[0], (), relay[0], (across,), ())
    own, _ = gather(pieces[1], before, (), direct[1], relay[1])

    def product(child, anc):
        return call(
            functools.partial(product_kernel, child),
            struct((SW, SW)),
            [VMEM] * 8,
            scratch=[pltpu.VMEM((SW, WIDE), BF16)] * 2,
        )(parts[child], *direct[child], *relay[child], *anc, meta)

    theirs = [product(0, other)]
    received = [step(theirs[0], "zl", 1, 2)]
    parts[1] = after(parts[1], theirs[0])
    theirs.append(product(1, other))
    received.append(step(theirs[1], "zl", 1, 2))
    mine = [product(child, own) for child in range(2)]

    packed = struct((10 * B, B))
    params = dict(
        grid=(1,),
        compiler_params=pltpu.CompilerParams(vmem_limit_bytes=LIMIT),
        cost_estimate=pl.CostEstimate(flops=1024, bytes_accessed=1024, transcendentals=0),
    )

    def block(child):
        return pl.BlockSpec((SW, SW), lambda g: (child, 0))

    anywhere = pl.BlockSpec(memory_space=pl.ANY)
    off, first = pl.pallas_call(
        functools.partial(finish_kernel, 0),
        out_shape=(struct(panel.shape), packed),
        in_specs=[VMEM, VMEM, block(0), VMEM],
        out_specs=[block(0), VMEM],
        **params,
    )(mine[0], received[0], panel, meta)
    second = call(functools.partial(update_kernel, 1), packed, [VMEM] * 5)(
        mine[1], theirs[1], parts[1], across, meta
    )
    off = pl.pallas_call(
        functools.partial(finish_kernel, 1),
        out_shape=struct(panel.shape),
        in_specs=[VMEM, VMEM, block(1), VMEM, anywhere],
        out_specs=block(1),
        input_output_aliases={4: 0},
        **params,
    )(mine[1], received[1], panel, meta, off)

    def swap(value):
        return lax.all_to_all(value, ROW, 0, 0, tiled=True)

    shape = (8, 20 * B // 8, B)
    spread = swap(jnp.concatenate([first, second], axis=0).reshape(shape))
    spread = after(spread, received[1])
    summed = swap(call(sum_kernel, struct(shape), [VMEM])(spread)).reshape(20, B, B)
    out = call(child_kernel, struct(diag_inverse.shape), [VMEM] * 3)(summed, diag_inverse, meta)
    return off, out


def solution(mesh):
    fine = Mesh(mesh.devices.reshape(2, 4, 2, 4, 4), ("core", "y", "zl", "zh", "x"))
    group = ("core", "zh", "x")
    in_specs = (P(ROW, group), P(group, ROW), P(group, None), P(), P())
    out_specs = (P(group, ROW), P(group, None))
    return jax.shard_map(local, mesh=fine, in_specs=in_specs, out_specs=out_specs, check_vma=False)
```

```python
import functools

import jax
import jax.numpy as jnp
from jax import lax
from jax.experimental import pallas as pl
from jax.experimental.pallas import tpu as pltpu
from jax.sharding import Mesh, PartitionSpec as P

B = 128
SW = 512
WIDE = 2048
LIMIT = 22 * 2**20
ROW = ("y", "zl")
Z = ("zl", "zh")
DIRECTIONS = (0, 3, 1, 2)

VMEM = pl.BlockSpec(memory_space=pltpu.VMEM)
SMEM = pl.BlockSpec(memory_space=pltpu.SMEM)
F32 = jnp.float32
BF16 = jnp.bfloat16


def call(kernel, out_shape, specs, out_specs=None, scratch=(), aliases=None):
    single = not isinstance(out_shape, (tuple, list))
    return pl.pallas_call(
        kernel,
        out_shape=out_shape,
        in_specs=specs,
        out_specs=out_specs if out_specs is not None else (VMEM if single else [VMEM] * len(out_shape)),
        scratch_shapes=list(scratch),
        input_output_aliases=aliases or {},
        compiler_params=pltpu.CompilerParams(vmem_limit_bytes=LIMIT),
        cost_estimate=pl.CostEstimate(flops=1024, bytes_accessed=1024, transcendentals=0),
    )


def struct(shape, dtype=F32):
    return jax.ShapeDtypeStruct(shape, dtype)


def z_rounds():
    even = [
        {0: 0, 2: 1, 4: 4, 6: 5},
        {6: 0, 0: 1, 2: 4, 4: 5},
        {2: 0, 4: 1, 6: 4, 0: 5},
        {4: 0, 6: 1, 0: 4, 2: 5},
    ]
    rounds = []
    table = {}
    for k, pairs in enumerate(even):
        pairs = {**pairs, **{(3 - t) % 8: (3 - s) % 8 for t, s in pairs.items()}}
        rounds.append([((s % 2) * 4 + s // 2, (t % 2) * 4 + t // 2) for t, s in pairs.items()])
        for t, s in pairs.items():
            table[t, int(s % 2 == t % 2), (s // 2) // 2] = k
    return rounds, table


def step(value, axis, k, n=4):
    return lax.ppermute(value, axis, [(i, (i + k) % n) for i in range(n)])


def split(value):
    high = value.astype(BF16)
    return high, (value - high.astype(F32)).astype(BF16)


def dot3(a, b):
    dims = (((1,), (1,)), ((), ()))
    mul = functools.partial(lax.dot_general, dimension_numbers=dims, preferred_element_type=F32)
    return mul(a[0], b[0]) + (mul(a[0], b[1]) + mul(a[1], b[0]))


def meta_kernel(ids, widths, pattern, out):
    core, y, zl, zh, x = (ids[i] for i in range(5))
    first = ((core * 4 + zh) * 4 + x) * 2
    for child in range(2):
        for d, shift in enumerate(DIRECTIONS):
            block = ((y + shift) % 4 * 2 + zl) * 4
            for k in range(4):
                value = pattern[first + child, block + k].astype(F32)
                out[child : child + 1, (d * 4 + k) * B : (d * 4 + k + 1) * B] = jnp.full((1, B), value)
        out[2 + child : 3 + child, :] = jnp.full((1, WIDE), (widths[first + child] * B).astype(F32))
    out[4:8, :] = jnp.zeros((4, WIDE), F32)


def column_mask(meta, child):
    position = lax.broadcasted_iota(jnp.int32, (SW, B), 0).astype(F32)
    return (position < meta[2 + child : 3 + child, :B]).astype(F32)


def prepare_kernel(table, ids, *refs):
    core, y, zl, zh, x = (ids[i] for i in range(5))
    mine, theirs, outs = refs[:5], refs[5:10], refs[10:]
    z = zh * 2 + zl
    for role in range(2):
        high, low = outs[2 * role : 2 * role + 2]
        places = [jnp.int32(0)] * 2
        for k in range(2):
            for at in range(8):
                places[k] = jnp.where(z == at, table[at, role, k], places[k])

        @pl.loop(0, 16)
        def _(i):
            d, k = i // 4, i % 4
            block = (y + jnp.where(d == 0, 0, jnp.where(d == 1, 3, jnp.where(d == 2, 1, 2)))) % 4
            place = jnp.where(block % 2 == 0, places[0], places[1])
            away = (k - x + 4) % 4
            lanes = pl.ds(pl.multiple_of(i * B, B), B)
            for here, pieces in ((block // 2 == core, mine), (block // 2 != core, theirs)):
                held, left, right, top, bottom = pieces
                for when, ref, at in (
                    (away == 0, held, place),
                    (away == 3, left, place),
                    (away == 1, right, place),
                    ((away == 2) & (place < 2), top, place % 2),
                    ((away == 2) & (place >= 2), bottom, place % 2),
                ):

                    @pl.when(here & when)
                    def _():
                        high[:, lanes], low[:, lanes] = split(ref[at])


def product_kernel(child, own, left, right, far, high, low, meta, out, phigh, plow):
    mask = column_mask(meta, child)
    rows = slice(child * SW, (child + 1) * SW)
    for d, source in enumerate((own, left, right, far)):
        for k in range(4):
            lanes = slice((d * 4 + k) * B, (d * 4 + k + 1) * B)
            here = slice(k * B, (k + 1) * B)
            value = source[:, here] if d == 3 else source[rows, here]
            phigh[:, lanes], plow[:, lanes] = split(value * mask * meta[child : child + 1, lanes])
    for n in range(0, 512, 256):
        b = (high[n : n + 256, :], low[n : n + 256, :])
        for r in range(0, SW, 256):
            out[r : r + 256, n : n + 256] = dot3((phigh[r : r + 256, :], plow[r : r + 256, :]), b)


def lower_blocks(update, left, right):
    at = 0
    for a in range(4):
        value = dot3([v[a * B : (a + 1) * B] for v in left], [v[: (a + 1) * B] for v in right])
        for b in range(a + 1):
            update[at * B : (at + 1) * B, :] = value[:, b * B : (b + 1) * B]
            at += 1


def finish_kernel(child, mine, received, panel, meta, *refs):
    off, update = refs[-2:]
    wide = jnp.concatenate([column_mask(meta, child)] * 4, axis=1)
    masks = wide * meta[child : child + 1, :SW]
    product = (mine[...] + received[...]) * masks
    off[...] = -product
    lower_blocks(update, split(product), split(panel[...] * masks))


def sum_kernel(parts, out):
    total = parts[0]
    for k in range(1, 8):
        total += parts[k]
    for k in range(8):
        out[k] = total


def child_kernel(child, parts, diag, meta, *refs):
    out = refs[-1]
    across = lax.broadcasted_iota(jnp.int32, (1, SW), 1).astype(F32) < meta[2 + child : 3 + child, :SW]
    across = across.astype(F32)
    mask = column_mask(meta, child)
    at = 0
    for a in range(4):
        for b in range(a + 1):
            block = parts[at]
            at += 1
            for (i, j), value in {(b, a): block.T, (a, b): block}.items():
                lines, lanes = slice(i * B, (i + 1) * B), slice(j * B, (j + 1) * B)
                out[lines, lanes] = (diag[lines, lanes] + value) * mask[lines] * across[:, lanes]


def after(value, *before):
    return lax.optimization_barrier((value, *before))[0]


def local(anc_inverse, panel, diag_inverse, widths, pattern):
    names = ("core", "y", "zl", "zh", "x")
    ids = jnp.stack([lax.axis_index(n) for n in names]).astype(jnp.int32)
    left, right = step(panel, "y", 1), step(panel, "y", -1)
    far = [step(left[:SW], "y", 1), step(right[SW:], "y", -1)]

    rounds, table = z_rounds()
    held = jnp.stack([lax.ppermute(anc_inverse, Z, pairs) for pairs in rounds])
    before, beyond = step(held, "x", 1), step(held, "x", -1)
    top, bottom = step(before[:2], "x", 1), step(beyond[2:], "x", -1)
    top = after(top, *far)
    pieces = [held, before, beyond, top, bottom]
    theirs = [step(value, "core", 1, 2) for value in pieces]
    anc = call(
        functools.partial(prepare_kernel, table), [struct((SW, WIDE), BF16)] * 4, [SMEM] + [VMEM] * 10
    )(ids, *pieces, *theirs)
    meta = call(meta_kernel, struct((8, WIDE)), [SMEM] * 3)(ids, widths, pattern)

    def product(child, role, panel):
        return call(
            functools.partial(product_kernel, child),
            struct((SW, SW)),
            [VMEM] * 7,
            scratch=[pltpu.VMEM((SW, WIDE), BF16)] * 2,
        )(panel, left, right, far[child], *anc[2 * role : 2 * role + 2], meta)

    sent = [product(0, 0, panel)]
    sent.append(product(1, 0, after(panel, sent[0])))
    received = [step(value, "zl", 1, 2) for value in sent]
    mine = [product(child, 1, after(panel, sent[1])) for child in range(2)]

    def swap(value):
        return lax.all_to_all(value, ROW, 0, 0, tiled=True)

    shape = (8, 10 * B // 8, B)
    off = out = None
    for child in range(2):
        block = pl.BlockSpec((SW, SW), lambda g, child=child: (child, 0))
        anywhere = [] if child == 0 else [pl.BlockSpec(memory_space=pl.ANY)]
        params = dict(
            grid=(1,),
            compiler_params=pltpu.CompilerParams(vmem_limit_bytes=LIMIT),
            cost_estimate=pl.CostEstimate(flops=1024, bytes_accessed=1024, transcendentals=0),
        )
        off, update = pl.pallas_call(
            functools.partial(finish_kernel, child),
            out_shape=(struct(panel.shape), struct((10 * B, B))),
            in_specs=[VMEM, VMEM, block, VMEM] + anywhere,
            out_specs=[block, VMEM],
            input_output_aliases={4: 0} if child else {},
            **params,
        )(mine[child], received[child], panel, meta, *([off] if child else []))
        summed = call(sum_kernel, struct(shape), [VMEM])(swap(update.reshape(shape)))
        summed = swap(summed).reshape(10, B, B)
        out = pl.pallas_call(
            functools.partial(child_kernel, child),
            out_shape=struct(diag_inverse.shape),
            in_specs=[VMEM, block, VMEM] + anywhere,
            out_specs=block,
            input_output_aliases={3: 0} if child else {},
            **params,
        )(summed, diag_inverse, meta, *([out] if child else []))
    return off, out


def solution(mesh):
    fine = Mesh(mesh.devices.reshape(2, 4, 2, 4, 4), ("core", "y", "zl", "zh", "x"))
    group = ("core", "zh", "x")
    in_specs = (P(ROW, group), P(group, ROW), P(group, None), P(), P())
    out_specs = (P(group, ROW), P(group, None))
    return jax.shard_map(local, mesh=fine, in_specs=in_specs, out_specs=out_specs, check_vma=False)
```

```python
import functools

import jax
import jax.numpy as jnp
from jax import lax
from jax.experimental import pallas as pl
from jax.experimental.pallas import tpu as pltpu
from jax.sharding import Mesh, PartitionSpec as P

B = 128
SW = 512
WIDE = 2048
LIMIT = 14 * 2**20
ROW = ("y", "zl")
Z = ("zl", "zh")
DIRECTIONS = (0, 3, 1, 2)

VMEM = pl.BlockSpec(memory_space=pltpu.VMEM)
SMEM = pl.BlockSpec(memory_space=pltpu.SMEM)
F32 = jnp.float32
BF16 = jnp.bfloat16


def call(kernel, out_shape, specs, out_specs=None, scratch=(), aliases=None):
    single = not isinstance(out_shape, (tuple, list))
    return pl.pallas_call(
        kernel,
        out_shape=out_shape,
        in_specs=specs,
        out_specs=out_specs if out_specs is not None else (VMEM if single else [VMEM] * len(out_shape)),
        scratch_shapes=list(scratch),
        input_output_aliases=aliases or {},
        compiler_params=pltpu.CompilerParams(vmem_limit_bytes=LIMIT),
        cost_estimate=pl.CostEstimate(flops=1024, bytes_accessed=1024, transcendentals=0),
    )


def struct(shape, dtype=F32):
    return jax.ShapeDtypeStruct(shape, dtype)


def z_rounds():
    even = [
        {0: 0, 2: 1, 4: 4, 6: 5},
        {6: 0, 0: 1, 2: 4, 4: 5},
        {2: 0, 4: 1, 6: 4, 0: 5},
        {4: 0, 6: 1, 0: 4, 2: 5},
    ]
    rounds = []
    table = {}
    for k, pairs in enumerate(even):
        pairs = {**pairs, **{(3 - t) % 8: (3 - s) % 8 for t, s in pairs.items()}}
        rounds.append([((s % 2) * 4 + s // 2, (t % 2) * 4 + t // 2) for t, s in pairs.items()])
        for t, s in pairs.items():
            table[t, int(s % 2 == t % 2), (s // 2) // 2] = k
    return rounds, table


def step(value, axis, k, n=4):
    return lax.ppermute(value, axis, [(i, (i + k) % n) for i in range(n)])


def split(value):
    high = value.astype(BF16)
    return high, (value - high.astype(F32)).astype(BF16)


def dot3(a, b):
    dims = (((1,), (1,)), ((), ()))
    mul = functools.partial(lax.dot_general, dimension_numbers=dims, preferred_element_type=F32)
    return mul(a[0], b[0]) + (mul(a[0], b[1]) + mul(a[1], b[0]))


def meta_kernel(ids, widths, pattern, out):
    core, y, zl, zh, x = (ids[i] for i in range(5))
    first = ((core * 4 + zh) * 4 + x) * 2
    for child in range(2):
        for d, shift in enumerate(DIRECTIONS):
            block = ((y + shift) % 4 * 2 + zl) * 4
            for k in range(4):
                value = pattern[first + child, block + k].astype(F32)
                out[child : child + 1, (d * 4 + k) * B : (d * 4 + k + 1) * B] = jnp.full((1, B), value)
        out[2 + child : 3 + child, :] = jnp.full((1, WIDE), (widths[first + child] * B).astype(F32))
        block = (y * 2 + 1 - zl) * 4
        for k in range(4):
            value = pattern[first + child, block + k].astype(F32)
            out[4 + child : 5 + child, k * B : (k + 1) * B] = jnp.full((1, B), value)
        out[4 + child : 5 + child, SW:] = jnp.zeros((1, WIDE - SW), F32)
    out[6:8, :] = jnp.zeros((2, WIDE), F32)


def column_mask(meta, child):
    position = lax.broadcasted_iota(jnp.int32, (SW, B), 0).astype(F32)
    return (position < meta[2 + child : 3 + child, :B]).astype(F32)


def select_kernel(table, ids, r0, r1, r2, r3, other, own):
    z = ids[3] * 2 + ids[2]
    for role, out in enumerate((other, own)):
        for k in range(2):
            place = jnp.int32(0)
            for at in range(8):
                place = jnp.where(z == at, table[at, role, k], place)
            for i, source in enumerate((r0, r1, r2, r3)):

                @pl.when(place == i)
                def _():
                    out[k] = source[...]


def each_piece(ids, body):
    @pl.loop(0, 16)
    def _(i):
        d, k = i // 4, i % 4
        block = (ids[1] + jnp.where(d == 0, 0, jnp.where(d == 1, 3, jnp.where(d == 2, 1, 2)))) % 4
        body(block, k, pl.ds(pl.multiple_of(i * B, B), B))


def sort_pieces_kernel(ids, *refs):
    mine, theirs, (high, low) = refs[:5], refs[5:10], refs[10:]

    def body(block, k, lanes):
        away, half = (k - ids[4] + 4) % 4, block % 2
        for here, pieces in ((block // 2 == ids[0], mine), (block // 2 != ids[0], theirs)):
            held, left, right, top, bottom = pieces
            for when, ref, at in (
                (away == 0, held, half),
                (away == 3, left, half),
                (away == 1, right, half),
                ((away == 2) & (half == 0), top, None),
                ((away == 2) & (half == 1), bottom, None),
            ):

                @pl.when(here & when)
                def _():
                    high[:, lanes], low[:, lanes] = split(ref[...] if at is None else ref[at])

    each_piece(ids, body)


def sort_gathered_kernel(ids, whole, high, low):
    def body(block, k, lanes):
        high[:, lanes], low[:, lanes] = split(whole[block // 2 * 4 + k, block % 2])

    each_piece(ids, body)


def product_kernel(child, own, left, right, left_tail, right_tail, top, bottom, high, low, meta, *refs):
    outs, (phigh, plow) = refs[:-2], refs[-2:]
    mask = column_mask(meta, child)
    rows = slice(child * SW, (child + 1) * SW)
    for d, source in enumerate((own, left, right, None)):
        for k in range(4):
            lanes = slice((d * 4 + k) * B, (d * 4 + k + 1) * B)
            here = slice(k * B, (k + 1) * B)
            if source is None:
                value = jnp.concatenate([top[:, here], bottom[:, here]], axis=0)
            elif d and child:
                end = (left_tail, right_tail)[d - 1]
                value = jnp.concatenate([source[SW:, here], end[:, here]], axis=0)
            else:
                value = source[rows, here]
            phigh[:, lanes], plow[:, lanes] = split(value * mask * meta[child : child + 1, lanes])
    for n in range(0, 512, 256):
        b = (high[n : n + 256, :], low[n : n + 256, :])
        for r in range(0, SW, 256):
            value = dot3((phigh[r : r + 256, :], plow[r : r + 256, :]), b)
            if len(outs) == 1:
                outs[0][r : r + 256, n : n + 256] = value
            else:
                outs[r // 256][:, n : n + 256] = value


def lower_blocks(update, pairs):
    at = 0
    for a in range(4):
        value = None
        for left, right in pairs:
            term = dot3([v[a * B : (a + 1) * B] for v in left], [v[: (a + 1) * B] for v in right])
            value = term if value is None else value + term
        for b in range(a + 1):
            update[at * B : (at + 1) * B, :] = value[:, b * B : (b + 1) * B]
            at += 1


def finish_kernel(child, mine, *refs):
    received, (panel, meta), refs = refs[: child + 1], refs[child + 1 : child + 3], refs[child + 3 :]
    wide = jnp.concatenate([column_mask(meta, child)] * 4, axis=1)
    masks = wide * meta[child : child + 1, :SW]
    product = (mine[...] + jnp.concatenate([ref[...] for ref in received], axis=0)) * masks
    if child == 0:
        off, update = refs
        lower_blocks(update, [(split(product), split(panel[...] * masks))])
    else:
        off = refs[-1]
    off[...] = -product


def update_kernel(child, mine, sent_top, sent_bottom, panel, across, meta, update):
    wide = jnp.concatenate([column_mask(meta, child)] * 4, axis=1)
    own = panel[child * SW : (child + 1) * SW, :] * wide * meta[child : child + 1, :SW]
    other = across[...] * wide * meta[4 + child : 5 + child, :SW]
    lower_blocks(update, [(split(mine[...]), split(own)), (split(jnp.concatenate([sent_top[...], sent_bottom[...]], axis=0)), split(other))])


def sum_kernel(parts, out):
    total = parts[0]
    for k in range(1, 8):
        total += parts[k]
    for k in range(8):
        out[k] = total


def child_kernel(parts, diag, meta, out):
    at = 0
    for child in range(2):
        across = lax.broadcasted_iota(jnp.int32, (1, SW), 1).astype(F32) < meta[2 + child : 3 + child, :SW]
        across = across.astype(F32)
        mask = column_mask(meta, child)
        for a in range(4):
            for b in range(a + 1):
                block = parts[at]
                at += 1
                for (i, j), value in {(b, a): block.T, (a, b): block}.items():
                    lines = slice(child * SW + i * B, child * SW + (i + 1) * B)
                    lanes = slice(j * B, (j + 1) * B)
                    rows = mask[i * B : (i + 1) * B]
                    out[lines, lanes] = (diag[lines, lanes] + value) * rows * across[:, lanes]


def after(value, *before):
    return lax.optimization_barrier((value, *before))[0]


def local(anc_inverse, panel, diag_inverse, widths, pattern):
    names = ("core", "y", "zl", "zh", "x")
    ids = jnp.stack([lax.axis_index(n) for n in names]).astype(jnp.int32)
    half, cut = SW // 2, SW + SW // 2
    head = [step(panel[:cut], "y", k) for k in (1, -1)]
    tail = [step(panel[cut:], "y", k) for k in (1, -1)]
    far = [
        (step(head[0][:half], "y", 1), step(head[1][half:SW], "y", -1)),
        (step(head[0][SW:cut], "y", 1), step(tail[1], "y", -1)),
    ]
    across = step(panel[SW:], "zl", 1, 2)

    rounds, table = z_rounds()
    got = [lax.ppermute(anc_inverse, Z, pairs) for pairs in rounds]
    got[0] = after(got[0], *head)
    piece = struct((2, SW, B))
    held, kept = call(functools.partial(select_kernel, table), (piece, piece), [SMEM] + [VMEM] * 4)(ids, *got)
    whole = lax.all_gather(kept, ("core", "x"), axis=0)
    before, beyond = step(held, "x", 1), step(held, "x", -1)
    top, bottom = step(after(before[0], *far[0]), "x", 1), step(after(beyond[1], *far[0]), "x", -1)
    top, bottom = after(top, *tail, across), after(bottom, *tail)
    pieces = [held, before, beyond, top, bottom]
    pieces += [step(value, "core", 1, 2) for value in pieces]
    pair = [struct((SW, WIDE), BF16)] * 2
    other = call(sort_pieces_kernel, pair, [SMEM] + [VMEM] * 10)(ids, *pieces)
    meta = call(meta_kernel, struct((8, WIDE)), [SMEM] * 3)(ids, widths, pattern)

    def product(child, anc, panel, pieces=1):
        return call(
            functools.partial(product_kernel, child),
            [struct((SW // pieces, SW))] * pieces,
            [VMEM] * 10,
            scratch=[pltpu.VMEM((SW, WIDE), BF16)] * 2,
        )(panel, *head, *tail, *far[child], *anc, meta)

    sent = product(0, other, panel)
    sent += product(1, other, after(panel, sent[0]), 2)
    received = [step(value, "zl", 1, 2) for value in sent]
    own = call(sort_gathered_kernel, pair, [SMEM, VMEM])(ids, after(whole, sent[1]))
    mine = [product(child, own, panel)[0] for child in range(2)]

    packed = struct((10 * B, B))
    params = dict(
        grid=(1,),
        compiler_params=pltpu.CompilerParams(vmem_limit_bytes=LIMIT),
        cost_estimate=pl.CostEstimate(flops=1024, bytes_accessed=1024, transcendentals=0),
    )
    blocks = [pl.BlockSpec((SW, SW), lambda g, child=child: (child, 0)) for child in range(2)]
    off, first = pl.pallas_call(
        functools.partial(finish_kernel, 0),
        out_shape=(struct(panel.shape), packed),
        in_specs=[VMEM, VMEM, blocks[0], VMEM],
        out_specs=[blocks[0], VMEM],
        **params,
    )(mine[0], received[0], panel, meta)
    second = call(functools.partial(update_kernel, 1), packed, [VMEM] * 6)(
        mine[1], *sent[1:], panel, across, meta
    )
    off = pl.pallas_call(
        functools.partial(finish_kernel, 1),
        out_shape=struct(panel.shape),
        in_specs=[VMEM] * 3 + [blocks[1], VMEM, pl.BlockSpec(memory_space=pl.ANY)],
        out_specs=blocks[1],
        input_output_aliases={5: 0},
        **params,
    )(mine[1], *received[1:], panel, meta, off)

    def swap(value):
        return lax.all_to_all(value, ROW, 0, 0, tiled=True)

    shape = (8, 20 * B // 8, B)
    second = after(second, received[1])
    spread = swap(jnp.concatenate([first, second], axis=0).reshape(shape))
    spread = after(spread, received[2])
    summed = swap(call(sum_kernel, struct(shape), [VMEM])(spread)).reshape(20, B, B)
    out = call(child_kernel, struct(diag_inverse.shape), [VMEM] * 3)(summed, diag_inverse, meta)
    return off, out


def solution(mesh):
    fine = Mesh(mesh.devices.reshape(2, 4, 2, 4, 4), ("core", "y", "zl", "zh", "x"))
    group = ("core", "zh", "x")
    in_specs = (P(ROW, group), P(group, ROW), P(group, None), P(), P())
    out_specs = (P(group, ROW), P(group, None))
    return jax.shard_map(local, mesh=fine, in_specs=in_specs, out_specs=out_specs, check_vma=False)
```

```python
import functools

import jax
import jax.numpy as jnp
from jax import lax
from jax.experimental import pallas as pl
from jax.experimental.pallas import tpu as pltpu
from jax.sharding import Mesh, PartitionSpec as P

B = 128
SW = 512
WIDE = 4096
LIMIT = 24 * 2**20
ROW = ("y", "zl")
GROUP = ("core", "zh", "x")
DIRECTIONS = ((0, 0), (3, 0), (1, 0), (0, 1), (3, 1), (1, 1), (2, 0), (2, 1))
CUTS = (0, 192, 352, 512)

VMEM = pl.BlockSpec(memory_space=pltpu.VMEM)
SMEM = pl.BlockSpec(memory_space=pltpu.SMEM)
F32 = jnp.float32
BF16 = jnp.bfloat16


def call(kernel, out_shape, specs, out_specs=None, scratch=(), aliases=None):
    single = not isinstance(out_shape, (tuple, list))
    return pl.pallas_call(
        kernel,
        out_shape=out_shape,
        in_specs=specs,
        out_specs=out_specs if out_specs is not None else (VMEM if single else [VMEM] * len(out_shape)),
        scratch_shapes=list(scratch),
        input_output_aliases=aliases or {},
        compiler_params=pltpu.CompilerParams(vmem_limit_bytes=LIMIT),
        cost_estimate=pl.CostEstimate(flops=1024, bytes_accessed=1024, transcendentals=0),
    )


def struct(shape, dtype=F32):
    return jax.ShapeDtypeStruct(shape, dtype)


def step(value, axis, k, n=4):
    return lax.ppermute(value, axis, [(i, (i + k) % n) for i in range(n)])


def split(value):
    high = value.astype(BF16)
    return high, (value - high.astype(F32)).astype(BF16)


def dot3(a, b):
    dims = (((1,), (1,)), ((), ()))
    mul = functools.partial(lax.dot_general, dimension_numbers=dims, preferred_element_type=F32)
    return mul(a[0], b[0]) + (mul(a[0], b[1]) + mul(a[1], b[0]))


def meta_kernel(ids, widths, pattern, out):
    core, y, zl, zh, x = (ids[i] for i in range(5))
    first = ((core * 4 + zh) * 4 + x) * 2
    for child in range(2):
        for d, (dy, dz) in enumerate(DIRECTIONS):
            block = ((y + dy) % 4 * 2 + (zl + dz) % 2) * 4
            for k in range(4):
                value = pattern[first + child, block + k].astype(F32)
                out[child : child + 1, (d * 4 + k) * B : (d * 4 + k + 1) * B] = jnp.full((1, B), value)
        out[2 + child : 3 + child, :] = jnp.full((1, WIDE), (widths[first + child] * B).astype(F32))
    out[4:8, :] = jnp.zeros((4, WIDE), F32)


def column_mask(meta, child):
    position = lax.broadcasted_iota(jnp.int32, (SW, B), 0).astype(F32)
    return (position < meta[2 + child : 3 + child, :B]).astype(F32)


def masks(meta, child, d):
    return jnp.concatenate([column_mask(meta, child)] * 4, axis=1) * meta[child : child + 1, d * SW : (d + 1) * SW]


def columns(ids, anc, d):
    dy, dz = DIRECTIONS[d]
    block = (ids[1] + dy) % 4 * 2 + (ids[2] + dz) % 2
    return split(anc[:, pl.ds(pl.multiple_of(block * SW, SW), SW)])


def first_kernel(ids, anc, *refs):
    panels, meta, out = refs[:4], refs[4], refs[5]
    for d, panel in enumerate(panels):
        right = columns(ids, anc, d)
        for child in range(2):
            rows = slice(child * SW, (child + 1) * SW)
            value = dot3(split(panel[rows] * masks(meta, child, d)), right)
            out[rows] = value if d == 0 else out[rows] + value


def second_kernel(ids, anc, total, *refs):
    panels, meta, (out, high, low) = refs[:3], refs[3], refs[4:]
    for d, panel in enumerate(panels, 4):
        right = columns(ids, anc, d)
        for child in range(2):
            rows = slice(child * SW, (child + 1) * SW)
            before = total[rows] if d == 4 else out[rows]
            out[rows] = before + dot3(split(panel[rows] * masks(meta, child, d)), right)
    high[...], low[...] = columns(ids, anc, 7)


def last_kernel(child, total, one, two, three, high, low, panel, meta, *refs):
    off, update = refs[-2:]
    value = jnp.concatenate([one[...], two[...], three[...]], axis=0)
    value = dot3(split(value * masks(meta, child, 7)), (high[...], low[...]))
    mask = masks(meta, child, 0)
    product = (total[...] + value) * mask
    off[...] = -product
    lower_blocks(update, [(split(product), split(panel[...] * mask))])


def lower_blocks(update, pairs):
    at = 0
    for a in range(4):
        value = None
        for left, right in pairs:
            term = dot3([v[a * B : (a + 1) * B] for v in left], [v[: (a + 1) * B] for v in right])
            value = term if value is None else value + term
        for b in range(a + 1):
            update[at * B : (at + 1) * B, :] = value[:, b * B : (b + 1) * B]
            at += 1


def sum_kernel(parts, out):
    total = parts[0]
    for k in range(1, 8):
        total += parts[k]
    for k in range(8):
        out[k] = total


def child_kernel(parts, diag, meta, out):
    at = 0
    for child in range(2):
        across = lax.broadcasted_iota(jnp.int32, (1, SW), 1).astype(F32) < meta[2 + child : 3 + child, :SW]
        across = across.astype(F32)
        mask = column_mask(meta, child)
        for a in range(4):
            for b in range(a + 1):
                block = parts[at]
                at += 1
                for (i, j), value in {(b, a): block.T, (a, b): block}.items():
                    lines = slice(child * SW + i * B, child * SW + (i + 1) * B)
                    lanes = slice(j * B, (j + 1) * B)
                    rows = mask[i * B : (i + 1) * B]
                    out[lines, lanes] = (diag[lines, lanes] + value) * rows * across[:, lanes]


def after(value, *before):
    return lax.optimization_barrier((value, *before))[0]


def local(anc_inverse, panel, diag_inverse, widths, pattern):
    names = ("core", "y", "zl", "zh", "x")
    ids = jnp.stack([lax.axis_index(n) for n in names]).astype(jnp.int32)
    meta = call(meta_kernel, struct((8, WIDE)), [SMEM] * 3)(ids, widths, pattern)
    anc = lax.all_gather(anc_inverse, GROUP, axis=1, tiled=True)

    left, right, across = step(panel, "y", 1), step(panel, "y", -1), step(panel, "zl", 1, 2)
    came, crossed = after(left, right, across), after(across, right, left)
    left_across, right_across, far = step(came, "zl", 1, 2), step(crossed, "y", -1), step(came, "y", 1)
    left_across, right_across, far = lax.optimization_barrier((left_across, right_across, far))
    last = []
    for first in (0, SW):
        one, two, three = (
            value[first + a : first + b]
            for value, a, b in zip((left_across, right_across, far), CUTS[:-1], CUTS[1:])
        )
        last.append((step(one, "y", 1), step(two, "y", -1), step(three, "zl", 1, 2)))
    anc = after(anc, left_across, right_across, far)

    total = struct(panel.shape)
    term = call(first_kernel, total, [SMEM] + [VMEM] * 6)(ids, anc, panel, left, right, across, meta)
    piece = struct((SW, SW), BF16)
    term, high, low = call(second_kernel, (total, piece, piece), [SMEM] + [VMEM] * 6)(
        ids, anc, term, left_across, right_across, far, meta
    )
    off, updates = None, []
    for child in range(2):
        block = pl.BlockSpec((SW, SW), lambda g, child=child: (child, 0))
        off, update = pl.pallas_call(
            functools.partial(last_kernel, child),
            grid=(1,),
            out_shape=(struct(panel.shape), struct((10 * B, B))),
            in_specs=[block] + [VMEM] * 5 + [block, VMEM] + [pl.BlockSpec(memory_space=pl.ANY)] * child,
            out_specs=[block, VMEM],
            input_output_aliases={8: 0} if child else {},
            compiler_params=pltpu.CompilerParams(vmem_limit_bytes=LIMIT),
            cost_estimate=pl.CostEstimate(flops=1024, bytes_accessed=1024, transcendentals=0),
        )(term, *last[child], high, low, panel, meta, *([off] if child else []))
        updates.append(update)

    def swap(value):
        return lax.all_to_all(value, ROW, 0, 0, tiled=True)

    shape = (8, 20 * B // 8, B)
    spread = swap(jnp.concatenate(updates, axis=0).reshape(shape))
    summed = swap(call(sum_kernel, struct(shape), [VMEM])(spread)).reshape(20, B, B)
    out = call(child_kernel, struct(diag_inverse.shape), [VMEM] * 3)(summed, diag_inverse, meta)
    return off, out


def solution(mesh):
    fine = Mesh(mesh.devices.reshape(2, 4, 2, 4, 4), ("core", "y", "zl", "zh", "x"))
    in_specs = (P(ROW, GROUP), P(GROUP, ROW), P(GROUP, None), P(), P())
    out_specs = (P(GROUP, ROW), P(GROUP, None))
    return jax.shard_map(local, mesh=fine, in_specs=in_specs, out_specs=out_specs, check_vma=False)
```

```python
import functools

import jax
import jax.numpy as jnp
from jax import lax
from jax.experimental import pallas as pl
from jax.experimental.pallas import tpu as pltpu
from jax.sharding import Mesh, PartitionSpec as P

B = 128
SW = 512
WIDE = 2048
LIMIT = 22 * 2**20
ROW = ("y", "zl")
Z = ("zl", "zh")
DIRECTIONS = (0, 3, 1, 2)

VMEM = pl.BlockSpec(memory_space=pltpu.VMEM)
SMEM = pl.BlockSpec(memory_space=pltpu.SMEM)
F32 = jnp.float32
BF16 = jnp.bfloat16


def call(kernel, out_shape, specs, out_specs=None, scratch=(), aliases=None):
    single = not isinstance(out_shape, (tuple, list))
    return pl.pallas_call(
        kernel,
        out_shape=out_shape,
        in_specs=specs,
        out_specs=out_specs if out_specs is not None else (VMEM if single else [VMEM] * len(out_shape)),
        scratch_shapes=list(scratch),
        input_output_aliases=aliases or {},
        compiler_params=pltpu.CompilerParams(vmem_limit_bytes=LIMIT),
        cost_estimate=pl.CostEstimate(flops=1024, bytes_accessed=1024, transcendentals=0),
    )


def struct(shape, dtype=F32):
    return jax.ShapeDtypeStruct(shape, dtype)


def z_rounds():
    even = [
        {0: 0, 2: 1, 4: 4, 6: 5},
        {6: 0, 0: 1, 2: 4, 4: 5},
        {2: 0, 4: 1, 6: 4, 0: 5},
        {4: 0, 6: 1, 0: 4, 2: 5},
    ]
    rounds = []
    table = {}
    for k, pairs in enumerate(even):
        pairs = {**pairs, **{(3 - t) % 8: (3 - s) % 8 for t, s in pairs.items()}}
        rounds.append([((s % 2) * 4 + s // 2, (t % 2) * 4 + t // 2) for t, s in pairs.items()])
        for t, s in pairs.items():
            table[t, int(s % 2 == t % 2), (s // 2) // 2] = k
    return rounds, table


def step(value, axis, k, n=4):
    return lax.ppermute(value, axis, [(i, (i + k) % n) for i in range(n)])


def split(value):
    high = value.astype(BF16)
    return high, (value - high.astype(F32)).astype(BF16)


def dot3(a, b):
    dims = (((1,), (1,)), ((), ()))
    mul = functools.partial(lax.dot_general, dimension_numbers=dims, preferred_element_type=F32)
    return mul(a[0], b[0]) + (mul(a[0], b[1]) + mul(a[1], b[0]))


def meta_kernel(ids, widths, pattern, out):
    core, y, zl, zh, x = (ids[i] for i in range(5))
    first = ((core * 4 + zh) * 4 + x) * 2
    for child in range(2):
        for d, shift in enumerate(DIRECTIONS):
            block = ((y + shift) % 4 * 2 + zl) * 4
            for k in range(4):
                value = pattern[first + child, block + k].astype(F32)
                out[child : child + 1, (d * 4 + k) * B : (d * 4 + k + 1) * B] = jnp.full((1, B), value)
        out[2 + child : 3 + child, :] = jnp.full((1, WIDE), (widths[first + child] * B).astype(F32))
    out[4:8, :] = jnp.zeros((4, WIDE), F32)


def column_mask(meta, child):
    position = lax.broadcasted_iota(jnp.int32, (SW, B), 0).astype(F32)
    return (position < meta[2 + child : 3 + child, :B]).astype(F32)


def place_of(table, ids, role, half):
    z = ids[3] * 2 + ids[2]
    places = [jnp.int32(0)] * 2
    for k in range(2):
        for at in range(8):
            places[k] = jnp.where(z == at, table[at, role, k], places[k])
    return jnp.where(half == 0, *places)


def each_block(table, ids, role, body):
    @pl.loop(0, 4)
    def _(d):
        block = (ids[1] + jnp.where(d == 0, 0, jnp.where(d == 1, 3, jnp.where(d == 2, 1, 2)))) % 4
        body(d, block // 2 == ids[0], place_of(table, ids, role, block % 2))


def near_kernel(table, ids, *refs):
    for role in range(2):
        high, low = refs[6 + 2 * role : 8 + 2 * role]

        def body(d, here, place):
            for a in range(3):
                lanes = pl.ds(pl.multiple_of((a * 4 + d) * B, B), B)
                for when, ref in ((here, refs[a]), (jnp.logical_not(here), refs[3 + a])):

                    @pl.when(when)
                    def _():
                        high[:, lanes], low[:, lanes] = split(ref[place])

        each_block(table, ids, role, body)


def far_kernel(table, role, ids, *refs):
    high, low = refs[4:]

    def body(d, here, place):
        lanes = pl.ds(pl.multiple_of(d * B, B), B)
        for core, when in ((0, here), (1, jnp.logical_not(here))):
            for side, where in ((0, place < 2), (1, place >= 2)):

                @pl.when(when & where)
                def _():
                    high[:, lanes], low[:, lanes] = split(refs[2 * core + side][place % 2])

    each_block(table, ids, role, body)


def product_kernel(child, ids, own, left, right, top, bottom, *refs):
    high, low, far_high, far_low, meta, out, phigh, plow = refs
    mask = column_mask(meta, child)
    rows = slice(child * SW, (child + 1) * SW)
    for a, away in enumerate((0, 3, 1, 2)):
        k = (ids[4] + away) % 4
        for d, source in enumerate((own, left, right, None)):
            here = pl.ds(pl.multiple_of(k * B, B), B)
            across = pl.ds(pl.multiple_of((d * 4 + k) * B, B), B)
            lanes = slice((a * 4 + d) * B, (a * 4 + d + 1) * B)
            if source is None:
                value = jnp.concatenate([top[:, here], bottom[:, here]], axis=0)
            else:
                value = source[rows, here]
            phigh[:, lanes], plow[:, lanes] = split(value * mask * meta[child : child + 1, across])
    near = 12 * B
    for n in range(0, SW, 256):
        lines = slice(n, n + 256)
        for r in range(0, SW, 256):
            at = slice(r, r + 256)
            value = dot3((phigh[at, :near], plow[at, :near]), (high[lines, :], low[lines, :]))
            value += dot3((phigh[at, near:], plow[at, near:]), (far_high[lines, :], far_low[lines, :]))
            out[at, lines] = value


def lower_blocks(update, left, right):
    at = 0
    for a in range(4):
        value = dot3([v[a * B : (a + 1) * B] for v in left], [v[: (a + 1) * B] for v in right])
        for b in range(a + 1):
            update[at * B : (at + 1) * B, :] = value[:, b * B : (b + 1) * B]
            at += 1


def finish_kernel(child, mine, received, panel, meta, *refs):
    off, update = refs[-2:]
    wide = jnp.concatenate([column_mask(meta, child)] * 4, axis=1)
    masks = wide * meta[child : child + 1, :SW]
    product = (mine[...] + received[...]) * masks
    off[...] = -product
    lower_blocks(update, split(product), split(panel[...] * masks))


def sum_kernel(parts, out):
    total = parts[0]
    for k in range(1, 8):
        total += parts[k]
    for k in range(8):
        out[k] = total


def child_kernel(parts, diag, meta, out):
    at = 0
    for child in range(2):
        across = lax.broadcasted_iota(jnp.int32, (1, SW), 1).astype(F32) < meta[2 + child : 3 + child, :SW]
        across = across.astype(F32)
        mask = column_mask(meta, child)
        for a in range(4):
            for b in range(a + 1):
                block = parts[at]
                at += 1
                for (i, j), value in {(b, a): block.T, (a, b): block}.items():
                    lines = slice(child * SW + i * B, child * SW + (i + 1) * B)
                    lanes = slice(j * B, (j + 1) * B)
                    rows = mask[i * B : (i + 1) * B]
                    out[lines, lanes] = (diag[lines, lanes] + value) * rows * across[:, lanes]


def after(value, *before):
    return lax.optimization_barrier((value, *before))[0]


def local(anc_inverse, panel, diag_inverse, widths, pattern):
    names = ("core", "y", "zl", "zh", "x")
    ids = jnp.stack([lax.axis_index(n) for n in names]).astype(jnp.int32)
    left, right = step(panel, "y", 1), step(panel, "y", -1)
    half = SW // 2
    far = [(step(left[a : a + half], "y", 1), step(right[a + half : a + SW], "y", -1)) for a in (0, SW)]

    rounds, table = z_rounds()
    held = jnp.stack([lax.ppermute(anc_inverse, Z, pairs) for pairs in rounds])
    before, beyond = step(held, "x", 1), step(held, "x", -1)
    near = [held, before, beyond]
    near += [step(value, "core", 1, 2) for value in near]
    ends = step(after(before[:2], *far[0]), "x", 1), step(after(beyond[2:], *far[0]), "x", -1)
    meta = call(meta_kernel, struct((8, WIDE)), [SMEM] * 3)(ids, widths, pattern)
    parts = call(
        functools.partial(near_kernel, table), [struct((SW, 12 * B), BF16)] * 4, [SMEM] + [VMEM] * 6
    )(ids, *near)
    ends = tuple(after(value, parts[0]) for value in ends)
    ends += tuple(step(value, "core", 1, 2) for value in ends)

    def product(role, first):
        pair = [struct((SW, SW), BF16)] * 2
        anc = call(functools.partial(far_kernel, table, role), pair, [SMEM] + [VMEM] * 4)(ids, first, *ends[1:])
        anc = (*parts[2 * role : 2 * role + 2], *anc)
        values = []
        for child in range(2):
            values.append(
                call(
                    functools.partial(product_kernel, child),
                    struct((SW, SW)),
                    [SMEM] + [VMEM] * 10,
                    scratch=[pltpu.VMEM((SW, WIDE), BF16)] * 2,
                )(ids, after(panel, *values) if values else panel, left, right, *far[child], *anc, meta)
            )
        return values

    sent = product(0, ends[0])
    received = [step(value, "zl", 1, 2) for value in sent]
    mine = product(1, after(ends[0], sent[1]))

    off, updates = None, []
    for child in range(2):
        block = pl.BlockSpec((SW, SW), lambda g, child=child: (child, 0))
        off, update = pl.pallas_call(
            functools.partial(finish_kernel, child),
            grid=(1,),
            out_shape=(struct(panel.shape), struct((10 * B, B))),
            in_specs=[VMEM, VMEM, block, VMEM] + [pl.BlockSpec(memory_space=pl.ANY)] * child,
            out_specs=[block, VMEM],
            input_output_aliases={4: 0} if child else {},
            compiler_params=pltpu.CompilerParams(vmem_limit_bytes=LIMIT),
            cost_estimate=pl.CostEstimate(flops=1024, bytes_accessed=1024, transcendentals=0),
        )(mine[child], received[child], panel, meta, *([off] if child else []))
        updates.append(update)

    def swap(value):
        return lax.all_to_all(value, ROW, 0, 0, tiled=True)

    shape = (8, 20 * B // 8, B)
    spread = swap(jnp.concatenate(updates, axis=0).reshape(shape))
    summed = swap(call(sum_kernel, struct(shape), [VMEM])(spread)).reshape(20, B, B)
    out = call(child_kernel, struct(diag_inverse.shape), [VMEM] * 3)(summed, diag_inverse, meta)
    return off, out


def solution(mesh):
    fine = Mesh(mesh.devices.reshape(2, 4, 2, 4, 4), ("core", "y", "zl", "zh", "x"))
    group = ("core", "zh", "x")
    in_specs = (P(ROW, group), P(group, ROW), P(group, None), P(), P())
    out_specs = (P(group, ROW), P(group, None))
    return jax.shard_map(local, mesh=fine, in_specs=in_specs, out_specs=out_specs, check_vma=False)
```

```python
import functools

import jax
import jax.numpy as jnp
from jax import lax
from jax.experimental import pallas as pl
from jax.experimental.pallas import tpu as pltpu
from jax.sharding import Mesh, PartitionSpec as P

B = 128
SW = 512
WIDE = 2048
LIMIT = 22 * 2**20
ROW = ("y", "zl")
Z = ("zl", "zh")
DIRECTIONS = (0, 3, 1, 2)

VMEM = pl.BlockSpec(memory_space=pltpu.VMEM)
SMEM = pl.BlockSpec(memory_space=pltpu.SMEM)
F32 = jnp.float32
BF16 = jnp.bfloat16


def call(kernel, out_shape, specs, out_specs=None, scratch=(), aliases=None):
    single = not isinstance(out_shape, (tuple, list))
    return pl.pallas_call(
        kernel,
        out_shape=out_shape,
        in_specs=specs,
        out_specs=out_specs if out_specs is not None else (VMEM if single else [VMEM] * len(out_shape)),
        scratch_shapes=list(scratch),
        input_output_aliases=aliases or {},
        compiler_params=pltpu.CompilerParams(vmem_limit_bytes=LIMIT),
        cost_estimate=pl.CostEstimate(flops=1024, bytes_accessed=1024, transcendentals=0),
    )


def struct(shape, dtype=F32):
    return jax.ShapeDtypeStruct(shape, dtype)


def z_rounds():
    even = [
        {0: 0, 2: 1, 4: 4, 6: 5},
        {6: 0, 0: 1, 2: 4, 4: 5},
        {2: 0, 4: 1, 6: 4, 0: 5},
        {4: 0, 6: 1, 0: 4, 2: 5},
    ]
    rounds = []
    table = {}
    for k, pairs in enumerate(even):
        pairs = {**pairs, **{(3 - t) % 8: (3 - s) % 8 for t, s in pairs.items()}}
        rounds.append([((s % 2) * 4 + s // 2, (t % 2) * 4 + t // 2) for t, s in pairs.items()])
        for t, s in pairs.items():
            table[t, int(s % 2 == t % 2), (s // 2) // 2] = k
    return rounds, table


def step(value, axis, k, n=4):
    return lax.ppermute(value, axis, [(i, (i + k) % n) for i in range(n)])


def split(value):
    high = value.astype(BF16)
    return high, (value - high.astype(F32)).astype(BF16)


def dot3(a, b):
    dims = (((1,), (1,)), ((), ()))
    mul = functools.partial(lax.dot_general, dimension_numbers=dims, preferred_element_type=F32)
    return mul(a[0], b[0]) + (mul(a[0], b[1]) + mul(a[1], b[0]))


def meta_kernel(ids, widths, pattern, out):
    core, y, zl, zh, x = (ids[i] for i in range(5))
    first = ((core * 4 + zh) * 4 + x) * 2
    for child in range(2):
        for d, shift in enumerate(DIRECTIONS):
            block = ((y + shift) % 4 * 2 + zl) * 4
            for k in range(4):
                value = pattern[first + child, block + k].astype(F32)
                out[child : child + 1, (d * 4 + k) * B : (d * 4 + k + 1) * B] = jnp.full((1, B), value)
        out[2 + child : 3 + child, :] = jnp.full((1, WIDE), (widths[first + child] * B).astype(F32))
    out[4:8, :] = jnp.zeros((4, WIDE), F32)


def column_mask(meta, child):
    position = lax.broadcasted_iota(jnp.int32, (SW, B), 0).astype(F32)
    return (position < meta[2 + child : 3 + child, :B]).astype(F32)


def place_of(table, ids, role, half):
    z = ids[3] * 2 + ids[2]
    places = [jnp.int32(0)] * 2
    for k in range(2):
        for at in range(8):
            places[k] = jnp.where(z == at, table[at, role, k], places[k])
    return jnp.where(half == 0, *places)


def each_block(table, ids, role, body):
    @pl.loop(0, 4)
    def _(d):
        block = (ids[1] + jnp.where(d == 0, 0, jnp.where(d == 1, 3, jnp.where(d == 2, 1, 2)))) % 4
        body(d, block // 2 == ids[0], place_of(table, ids, role, block % 2))


def near_kernel(table, ids, *refs):
    for role in range(2):
        high, low = refs[6 + 2 * role : 8 + 2 * role]

        def body(d, here, place):
            for a in range(3):
                lanes = pl.ds(pl.multiple_of((a * 4 + d) * B, B), B)
                for when, ref in ((here, refs[a]), (jnp.logical_not(here), refs[3 + a])):

                    @pl.when(when)
                    def _():
                        high[:, lanes], low[:, lanes] = split(ref[place])

        each_block(table, ids, role, body)


def far_kernel(table, role, ids, *refs):
    high, low = refs[4:]

    def body(d, here, place):
        lanes = pl.ds(pl.multiple_of(d * B, B), B)
        for core, when in ((0, here), (1, jnp.logical_not(here))):
            for side, where in ((0, place < 2), (1, place >= 2)):

                @pl.when(when & where)
                def _():
                    high[:, lanes], low[:, lanes] = split(refs[2 * core + side][place % 2])

    each_block(table, ids, role, body)


def product_kernel(child, ids, own, left, right, top, bottom, *refs):
    high, low, far_high, far_low, meta, out, phigh, plow = refs
    mask = column_mask(meta, child)
    for a, away in enumerate((0, 3, 1, 2)):
        k = (ids[4] + away) % 4
        for d, source in enumerate((own, left, right, None)):
            here = pl.ds(pl.multiple_of(k * B, B), B)
            across = pl.ds(pl.multiple_of((d * 4 + k) * B, B), B)
            lanes = slice((a * 4 + d) * B, (a * 4 + d + 1) * B)
            if source is None:
                value = jnp.concatenate([top[:, here], bottom[:, here]], axis=0)
            else:
                value = source[:, here]
            phigh[:, lanes], plow[:, lanes] = split(value * mask * meta[child : child + 1, across])
    near = 12 * B
    for n in range(0, SW, 256):
        lines = slice(n, n + 256)
        for r in range(0, SW, 256):
            at = slice(r, r + 256)
            value = dot3((phigh[at, :near], plow[at, :near]), (high[lines, :], low[lines, :]))
            value += dot3((phigh[at, near:], plow[at, near:]), (far_high[lines, :], far_low[lines, :]))
            out[at, lines] = value


def lower_blocks(update, left, right):
    at = 0
    for a in range(4):
        value = dot3([v[a * B : (a + 1) * B] for v in left], [v[: (a + 1) * B] for v in right])
        for b in range(a + 1):
            update[at * B : (at + 1) * B, :] = value[:, b * B : (b + 1) * B]
            at += 1


def finish_kernel(child, mine, received, panel, meta, *refs):
    off, update = refs[-2:]
    wide = jnp.concatenate([column_mask(meta, child)] * 4, axis=1)
    masks = wide * meta[child : child + 1, :SW]
    product = (mine[...] + received[...]) * masks
    off[...] = -product
    lower_blocks(update, split(product), split(panel[...] * masks))


def sum_kernel(parts, out):
    total = parts[0]
    for k in range(1, 8):
        total += parts[k]
    for k in range(8):
        out[k] = total


def child_kernel(parts, diag, meta, out):
    at = 0
    for child in range(2):
        across = lax.broadcasted_iota(jnp.int32, (1, SW), 1).astype(F32) < meta[2 + child : 3 + child, :SW]
        across = across.astype(F32)
        mask = column_mask(meta, child)
        for a in range(4):
            for b in range(a + 1):
                block = parts[at]
                at += 1
                for (i, j), value in {(b, a): block.T, (a, b): block}.items():
                    lines = slice(child * SW + i * B, child * SW + (i + 1) * B)
                    lanes = slice(j * B, (j + 1) * B)
                    rows = mask[i * B : (i + 1) * B]
                    out[lines, lanes] = (diag[lines, lanes] + value) * rows * across[:, lanes]


def after(value, *before):
    return lax.optimization_barrier((value, *before))[0]


def local(anc_inverse, panel, diag_inverse, widths, pattern):
    names = ("core", "y", "zl", "zh", "x")
    ids = jnp.stack([lax.axis_index(n) for n in names]).astype(jnp.int32)
    meta = call(meta_kernel, struct((8, WIDE)), [SMEM] * 3)(ids, widths, pattern)
    left, right = step(panel, "y", 1), step(panel, "y", -1)
    half = SW // 2
    far = [(step(left[a : a + half], "y", 1), step(right[a + half : a + SW], "y", -1)) for a in (0, SW)]

    rounds, table = z_rounds()
    got = [None if k == 1 else lax.ppermute(anc_inverse, Z, rounds[k]) for k in range(4)]
    got[1] = lax.ppermute(after(anc_inverse, got[0]), Z, rounds[1])
    held = jnp.stack(got)
    before, beyond = step(held, "x", 1), step(held, "x", -1)
    near = [after(held, meta), before, beyond]
    near += [step(value, "core", 1, 2) for value in near]
    ends = step(after(before[:2], *far[0]), "x", 1), step(after(beyond[2:], *far[0]), "x", -1)
    parts = call(
        functools.partial(near_kernel, table), [struct((SW, 12 * B), BF16)] * 4, [SMEM] + [VMEM] * 6
    )(ids, *near)
    ends = tuple(after(value, parts[0]) for value in ends)
    ends += tuple(step(value, "core", 1, 2) for value in ends)

    def product(role, first):
        pair = [struct((SW, SW), BF16)] * 2
        anc = call(functools.partial(far_kernel, table, role), pair, [SMEM] + [VMEM] * 4)(ids, first, *ends[1:])
        anc = (*parts[2 * role : 2 * role + 2], *anc)
        values = []
        for child in range(2):
            block = pl.BlockSpec((SW, SW), lambda g, child=child: (child, 0))
            values.append(
                pl.pallas_call(
                    functools.partial(product_kernel, child),
                    grid=(1,),
                    out_shape=struct((SW, SW)),
                    in_specs=[SMEM] + [block] * 3 + [VMEM] * 7,
                    out_specs=VMEM,
                    scratch_shapes=[pltpu.VMEM((SW, WIDE), BF16)] * 2,
                    compiler_params=pltpu.CompilerParams(vmem_limit_bytes=36 * 2**20),
                    cost_estimate=pl.CostEstimate(flops=1024, bytes_accessed=1024, transcendentals=0),
                )(ids, after(panel, *values) if values else panel, left, right, *far[child], *anc, meta)
            )
        return values

    sent = product(0, ends[0])
    received = [step(value, "zl", 1, 2) for value in sent]
    mine = product(1, after(ends[0], sent[1]))

    off, updates = None, []
    for child in range(2):
        block = pl.BlockSpec((SW, SW), lambda g, child=child: (child, 0))
        off, update = pl.pallas_call(
            functools.partial(finish_kernel, child),
            grid=(1,),
            out_shape=(struct(panel.shape), struct((10 * B, B))),
            in_specs=[VMEM, VMEM, block, VMEM] + [pl.BlockSpec(memory_space=pl.ANY)] * child,
            out_specs=[block, VMEM],
            input_output_aliases={4: 0} if child else {},
            compiler_params=pltpu.CompilerParams(vmem_limit_bytes=LIMIT),
            cost_estimate=pl.CostEstimate(flops=1024, bytes_accessed=1024, transcendentals=0),
        )(mine[child], received[child], panel, meta, *([off] if child else []))
        updates.append(update)

    def swap(value):
        return lax.all_to_all(value, ROW, 0, 0, tiled=True)

    shape = (8, 20 * B // 8, B)
    spread = swap(jnp.concatenate(updates, axis=0).reshape(shape))
    summed = swap(call(sum_kernel, struct(shape), [VMEM])(spread)).reshape(20, B, B)
    out = call(child_kernel, struct(diag_inverse.shape), [VMEM] * 3)(summed, diag_inverse, meta)
    return off, out


def solution(mesh):
    fine = Mesh(mesh.devices.reshape(2, 4, 2, 4, 4), ("core", "y", "zl", "zh", "x"))
    group = ("core", "zh", "x")
    in_specs = (P(ROW, group), P(group, ROW), P(group, None), P(), P())
    out_specs = (P(group, ROW), P(group, None))
    return jax.shard_map(local, mesh=fine, in_specs=in_specs, out_specs=out_specs, check_vma=False)
```

```python
import functools

import jax
import jax.numpy as jnp
from jax import lax
from jax.experimental import pallas as pl
from jax.experimental.pallas import tpu as pltpu
from jax.sharding import Mesh, PartitionSpec as P

B = 128
SW = 512
WIDE = 2048
LIMIT = 22 * 2**20
ROW = ("y", "zl")
Z = ("zl", "zh")
DIRECTIONS = (0, 3, 1, 2)

VMEM = pl.BlockSpec(memory_space=pltpu.VMEM)
SMEM = pl.BlockSpec(memory_space=pltpu.SMEM)
F32 = jnp.float32
BF16 = jnp.bfloat16


def call(kernel, out_shape, specs, out_specs=None, scratch=(), aliases=None):
    single = not isinstance(out_shape, (tuple, list))
    return pl.pallas_call(
        kernel,
        out_shape=out_shape,
        in_specs=specs,
        out_specs=out_specs if out_specs is not None else (VMEM if single else [VMEM] * len(out_shape)),
        scratch_shapes=list(scratch),
        input_output_aliases=aliases or {},
        compiler_params=pltpu.CompilerParams(vmem_limit_bytes=LIMIT),
        cost_estimate=pl.CostEstimate(flops=1024, bytes_accessed=1024, transcendentals=0),
    )


def struct(shape, dtype=F32):
    return jax.ShapeDtypeStruct(shape, dtype)


def z_rounds():
    even = [
        {0: 0, 2: 1, 4: 4, 6: 5},
        {6: 0, 0: 1, 2: 4, 4: 5},
        {2: 0, 4: 1, 6: 4, 0: 5},
        {4: 0, 6: 1, 0: 4, 2: 5},
    ]
    rounds = []
    table = {}
    for k, pairs in enumerate(even):
        pairs = {**pairs, **{(3 - t) % 8: (3 - s) % 8 for t, s in pairs.items()}}
        rounds.append([((s % 2) * 4 + s // 2, (t % 2) * 4 + t // 2) for t, s in pairs.items()])
        for t, s in pairs.items():
            table[t, int(s % 2 == t % 2), (s // 2) // 2] = k
    return rounds, table


def step(value, axis, k, n=4):
    return lax.ppermute(value, axis, [(i, (i + k) % n) for i in range(n)])


def split(value):
    high = value.astype(BF16)
    return high, (value - high.astype(F32)).astype(BF16)


def dot3(a, b):
    dims = (((1,), (1,)), ((), ()))
    mul = functools.partial(lax.dot_general, dimension_numbers=dims, preferred_element_type=F32)
    return mul(a[0], b[0]) + (mul(a[0], b[1]) + mul(a[1], b[0]))


def meta_kernel(ids, widths, pattern, out):
    core, y, zl, zh, x = (ids[i] for i in range(5))
    first = ((core * 4 + zh) * 4 + x) * 2
    for child in range(2):
        for d, shift in enumerate(DIRECTIONS):
            block = ((y + shift) % 4 * 2 + zl) * 4
            for k in range(4):
                value = pattern[first + child, block + k].astype(F32)
                out[child : child + 1, (d * 4 + k) * B : (d * 4 + k + 1) * B] = jnp.full((1, B), value)
        out[2 + child : 3 + child, :] = jnp.full((1, WIDE), (widths[first + child] * B).astype(F32))
    out[4:8, :] = jnp.zeros((4, WIDE), F32)


def column_mask(meta, child):
    position = lax.broadcasted_iota(jnp.int32, (SW, B), 0).astype(F32)
    return (position < meta[2 + child : 3 + child, :B]).astype(F32)


def select_kernel(table, ids, rounds, other, own, both):
    z = ids[3] * 2 + ids[2]
    for role, out in enumerate((other, own)):
        for k in range(2):
            place = jnp.int32(0)
            for at in range(8):
                place = jnp.where(z == at, table[at, role, k], place)
            value = rounds[place]
            out[k] = value
            both[2 * role + k] = value


def each_block(ids, body):
    @pl.loop(0, 4)
    def _(d):
        block = (ids[1] + jnp.where(d == 0, 0, jnp.where(d == 1, 3, jnp.where(d == 2, 1, 2)))) % 4
        body(d, block // 2 == ids[0], block % 2)


def near_kernel(role, ids, held, left, right, held_there, left_there, right_there, high, low):
    here_refs, there_refs = (held, left, right), (held_there, left_there, right_there)

    def body(d, here, half):
        for a in range(3):
            lanes = pl.ds(pl.multiple_of((a * 4 + d) * B, B), B)
            for when, refs in ((here, here_refs), (jnp.logical_not(here), there_refs)):

                @pl.when(when)
                def _():
                    at = half + 2 * role if a == 0 else half
                    high[:, lanes], low[:, lanes] = split(refs[a][at])

    each_block(ids, body)


def far_kernel(ids, *refs):
    high, low = refs[4:]

    def body(d, here, half):
        lanes = pl.ds(pl.multiple_of(d * B, B), B)
        for core, when in ((0, here), (1, jnp.logical_not(here))):
            for side in range(2):

                @pl.when(when & (half == side))
                def _():
                    high[:, lanes], low[:, lanes] = split(refs[2 * core + side][...])

    each_block(ids, body)


def product_kernel(child, ids, own, left, right, top, bottom, *refs):
    high, low, far_high, far_low, meta, out, phigh, plow = refs
    mask = column_mask(meta, child)
    for a, away in enumerate((0, 3, 1, 2)):
        k = (ids[4] + away) % 4
        for d, source in enumerate((own, left, right, None)):
            here = pl.ds(pl.multiple_of(k * B, B), B)
            across = pl.ds(pl.multiple_of((d * 4 + k) * B, B), B)
            lanes = slice((a * 4 + d) * B, (a * 4 + d + 1) * B)
            if source is None:
                value = jnp.concatenate([top[:, here], bottom[:, here]], axis=0)
            else:
                value = source[:, here]
            phigh[:, lanes], plow[:, lanes] = split(value * mask * meta[child : child + 1, across])
    near = 12 * B
    for n in range(0, SW, 256):
        lines = slice(n, n + 256)
        for r in range(0, SW, 256):
            at = slice(r, r + 256)
            value = dot3((phigh[at, :near], plow[at, :near]), (high[lines, :], low[lines, :]))
            value += dot3((phigh[at, near:], plow[at, near:]), (far_high[lines, :], far_low[lines, :]))
            out[at, lines] = value


def lower_blocks(update, left, right):
    at = 0
    for a in range(4):
        value = dot3([v[a * B : (a + 1) * B] for v in left], [v[: (a + 1) * B] for v in right])
        for b in range(a + 1):
            update[at * B : (at + 1) * B, :] = value[:, b * B : (b + 1) * B]
            at += 1


def finish_kernel(child, mine, received, panel, meta, *refs):
    off, update = refs[-2:]
    wide = jnp.concatenate([column_mask(meta, child)] * 4, axis=1)
    masks = wide * meta[child : child + 1, :SW]
    product = (mine[...] + received[...]) * masks
    off[...] = -product
    lower_blocks(update, split(product), split(panel[...] * masks))


def sum_kernel(parts, out):
    total = parts[0]
    for k in range(1, 8):
        total += parts[k]
    for k in range(8):
        out[k] = total


def child_kernel(parts, diag, meta, out):
    at = 0
    for child in range(2):
        across = lax.broadcasted_iota(jnp.int32, (1, SW), 1).astype(F32) < meta[2 + child : 3 + child, :SW]
        across = across.astype(F32)
        mask = column_mask(meta, child)
        for a in range(4):
            for b in range(a + 1):
                block = parts[at]
                at += 1
                for (i, j), value in {(b, a): block.T, (a, b): block}.items():
                    lines = slice(child * SW + i * B, child * SW + (i + 1) * B)
                    lanes = slice(j * B, (j + 1) * B)
                    rows = mask[i * B : (i + 1) * B]
                    out[lines, lanes] = (diag[lines, lanes] + value) * rows * across[:, lanes]


def after(value, *before):
    return lax.optimization_barrier((value, *before))[0]


def local(anc_inverse, panel, diag_inverse, widths, pattern):
    names = ("core", "y", "zl", "zh", "x")
    ids = jnp.stack([lax.axis_index(n) for n in names]).astype(jnp.int32)
    meta = call(meta_kernel, struct((8, WIDE)), [SMEM] * 3)(ids, widths, pattern)
    left, right = step(panel, "y", 1), step(panel, "y", -1)
    half = SW // 2
    far = [(step(left[a : a + half], "y", 1), step(right[a + half : a + SW], "y", -1)) for a in (0, SW)]

    rounds, table = z_rounds()
    got = [None if k == 1 else lax.ppermute(anc_inverse, Z, rounds[k]) for k in range(4)]
    got[1] = lax.ppermute(after(anc_inverse, got[0]), Z, rounds[1])
    piece = struct((2, SW, B))
    *held, both = call(
        functools.partial(select_kernel, table), (piece, piece, struct((4, SW, B))), [SMEM, VMEM]
    )(ids, jnp.stack(got))
    both = after(both, meta)
    there = step(both, "core", 1, 2)

    def around(value):
        return step(value, "x", 1), step(value, "x", -1)

    def opposite(before, beyond):
        return step(before[0], "x", 1), step(beyond[1], "x", -1)

    def cores(values):
        return [step(value, "core", 1, 2) for value in values]

    def near(role, sides):
        pair = [struct((SW, 12 * B), BF16)] * 2
        return call(functools.partial(near_kernel, role), pair, [SMEM] + [VMEM] * 6)(
            ids, both, *sides, there, *cores(sides)
        )

    sides = around(held[0])
    ends = opposite(*sides)
    second_sides = around(after(held[1], *sides))
    parts = near(0, sides)
    ends = [after(value, parts[0], *far[0]) for value in ends]

    def product(parts, ends, last):
        pair = [struct((SW, SW), BF16)] * 2
        anc = (*parts, *call(far_kernel, pair, [SMEM] + [VMEM] * 4)(ids, *ends, *cores(ends)))
        values = []
        for child in range(2):
            block = pl.BlockSpec((SW, SW), lambda g, child=child: (child, 0))
            values.append(
                pl.pallas_call(
                    functools.partial(product_kernel, child),
                    grid=(1,),
                    out_shape=struct((SW, SW)),
                    in_specs=[SMEM] + [block] * 3 + [VMEM] * 7,
                    out_specs=VMEM,
                    scratch_shapes=[pltpu.VMEM((SW, WIDE), BF16)] * 2,
                    compiler_params=pltpu.CompilerParams(vmem_limit_bytes=36 * 2**20),
                    cost_estimate=pl.CostEstimate(flops=1024, bytes_accessed=1024, transcendentals=0),
                )(ids, after(panel, *values, *last) if values else panel, left, right, *far[child], *anc, meta)
            )
        return values

    sent = product(parts, ends, second_sides)
    received = [step(value, "zl", 1, 2) for value in sent]
    ends = opposite(*second_sides)
    mine = product(near(1, second_sides), [after(value, sent[1]) for value in ends], ())

    off, updates = None, []
    for child in range(2):
        block = pl.BlockSpec((SW, SW), lambda g, child=child: (child, 0))
        off, update = pl.pallas_call(
            functools.partial(finish_kernel, child),
            grid=(1,),
            out_shape=(struct(panel.shape), struct((10 * B, B))),
            in_specs=[VMEM, VMEM, block, VMEM] + [pl.BlockSpec(memory_space=pl.ANY)] * child,
            out_specs=[block, VMEM],
            input_output_aliases={4: 0} if child else {},
            compiler_params=pltpu.CompilerParams(vmem_limit_bytes=LIMIT),
            cost_estimate=pl.CostEstimate(flops=1024, bytes_accessed=1024, transcendentals=0),
        )(mine[child], received[child], panel, meta, *([off] if child else []))
        updates.append(update)

    def swap(value):
        return lax.all_to_all(value, ROW, 0, 0, tiled=True)

    shape = (8, 20 * B // 8, B)
    spread = swap(jnp.concatenate(updates, axis=0).reshape(shape))
    summed = swap(call(sum_kernel, struct(shape), [VMEM])(spread)).reshape(20, B, B)
    out = call(child_kernel, struct(diag_inverse.shape), [VMEM] * 3)(summed, diag_inverse, meta)
    return off, out


def solution(mesh):
    fine = Mesh(mesh.devices.reshape(2, 4, 2, 4, 4), ("core", "y", "zl", "zh", "x"))
    group = ("core", "zh", "x")
    in_specs = (P(ROW, group), P(group, ROW), P(group, None), P(), P())
    out_specs = (P(group, ROW), P(group, None))
    return jax.shard_map(local, mesh=fine, in_specs=in_specs, out_specs=out_specs, check_vma=False)
```

```python
import functools

import jax
import jax.numpy as jnp
from jax import lax
from jax.experimental import pallas as pl
from jax.experimental.pallas import tpu as pltpu
from jax.sharding import Mesh, PartitionSpec as P

B = 128
SW = 512
WIDE = 2048
LIMIT = 22 * 2**20
ROW = ("y", "zl")
Z = ("zl", "zh")
DIRECTIONS = (0, 3, 1, 2)

VMEM = pl.BlockSpec(memory_space=pltpu.VMEM)
SMEM = pl.BlockSpec(memory_space=pltpu.SMEM)
F32 = jnp.float32
BF16 = jnp.bfloat16


def call(kernel, out_shape, specs, out_specs=None, scratch=(), aliases=None):
    single = not isinstance(out_shape, (tuple, list))
    return pl.pallas_call(
        kernel,
        out_shape=out_shape,
        in_specs=specs,
        out_specs=out_specs if out_specs is not None else (VMEM if single else [VMEM] * len(out_shape)),
        scratch_shapes=list(scratch),
        input_output_aliases=aliases or {},
        compiler_params=pltpu.CompilerParams(vmem_limit_bytes=LIMIT),
        cost_estimate=pl.CostEstimate(flops=1024, bytes_accessed=1024, transcendentals=0),
    )


def struct(shape, dtype=F32):
    return jax.ShapeDtypeStruct(shape, dtype)


def z_rounds():
    even = [
        {0: 0, 2: 1, 4: 4, 6: 5},
        {6: 0, 0: 1, 2: 4, 4: 5},
        {2: 0, 4: 1, 6: 4, 0: 5},
        {4: 0, 6: 1, 0: 4, 2: 5},
    ]
    rounds = []
    table = {}
    for k, pairs in enumerate(even):
        pairs = {**pairs, **{(3 - t) % 8: (3 - s) % 8 for t, s in pairs.items()}}
        rounds.append([((s % 2) * 4 + s // 2, (t % 2) * 4 + t // 2) for t, s in pairs.items()])
        for t, s in pairs.items():
            table[t, int(s % 2 == t % 2), (s // 2) // 2] = k
    return rounds, table


def step(value, axis, k, n=4):
    return lax.ppermute(value, axis, [(i, (i + k) % n) for i in range(n)])


def split(value):
    high = value.astype(BF16)
    return high, (value - high.astype(F32)).astype(BF16)


def dot3(a, b):
    dims = (((1,), (1,)), ((), ()))
    mul = functools.partial(lax.dot_general, dimension_numbers=dims, preferred_element_type=F32)
    return mul(a[0], b[0]) + (mul(a[0], b[1]) + mul(a[1], b[0]))


def meta_kernel(ids, widths, pattern, out):
    core, y, zl, zh, x = (ids[i] for i in range(5))
    first = ((core * 4 + zh) * 4 + x) * 2
    for child in range(2):
        for d, shift in enumerate(DIRECTIONS):
            block = ((y + shift) % 4 * 2 + zl) * 4
            for k in range(4):
                value = pattern[first + child, block + k].astype(F32)
                out[child : child + 1, (d * 4 + k) * B : (d * 4 + k + 1) * B] = jnp.full((1, B), value)
        out[2 + child : 3 + child, :] = jnp.full((1, WIDE), (widths[first + child] * B).astype(F32))
    out[4:8, :] = jnp.zeros((4, WIDE), F32)


def column_mask(meta, child):
    position = lax.broadcasted_iota(jnp.int32, (SW, B), 0).astype(F32)
    return (position < meta[2 + child : 3 + child, :B]).astype(F32)


def place_of(table, ids, role, half):
    z = ids[3] * 2 + ids[2]
    places = [jnp.int32(0)] * 2
    for k in range(2):
        for at in range(8):
            places[k] = jnp.where(z == at, table[at, role, k], places[k])
    return jnp.where(half == 0, *places)


def each_block(table, ids, role, body):
    @pl.loop(0, 4)
    def _(d):
        block = (ids[1] + jnp.where(d == 0, 0, jnp.where(d == 1, 3, jnp.where(d == 2, 1, 2)))) % 4
        body(d, block // 2 == ids[0], place_of(table, ids, role, block % 2))


def near_kernel(table, ids, *refs):
    for role in range(2):
        high, low = refs[6 + 2 * role : 8 + 2 * role]

        def body(d, here, place):
            for a in range(3):
                lanes = pl.ds(pl.multiple_of((a * 4 + d) * B, B), B)
                for when, ref in ((here, refs[a]), (jnp.logical_not(here), refs[3 + a])):

                    @pl.when(when)
                    def _():
                        high[:, lanes], low[:, lanes] = split(ref[place])

        each_block(table, ids, role, body)


def far_kernel(table, role, ids, *refs):
    high, low = refs[4:]

    def body(d, here, place):
        lanes = pl.ds(pl.multiple_of(d * B, B), B)
        for core, when in ((0, here), (1, jnp.logical_not(here))):
            for side, where in ((0, place < 2), (1, place >= 2)):

                @pl.when(when & where)
                def _():
                    high[:, lanes], low[:, lanes] = split(refs[2 * core + side][place % 2])

    each_block(table, ids, role, body)


def product_kernel(child, ids, own, left, right, top, bottom, *refs):
    high, low, far_high, far_low, meta, out, phigh, plow = refs
    mask = column_mask(meta, child)
    for a, away in enumerate((0, 3, 1, 2)):
        k = (ids[4] + away) % 4
        for d, source in enumerate((own, left, right, None)):
            here = pl.ds(pl.multiple_of(k * B, B), B)
            across = pl.ds(pl.multiple_of((d * 4 + k) * B, B), B)
            lanes = slice((a * 4 + d) * B, (a * 4 + d + 1) * B)
            if source is None:
                value = jnp.concatenate([top[:, here], bottom[:, here]], axis=0)
            else:
                value = source[:, here]
            phigh[:, lanes], plow[:, lanes] = split(value * mask * meta[child : child + 1, across])
    near = 12 * B
    for n in range(0, SW, 256):
        lines = slice(n, n + 256)
        for r in range(0, SW, 256):
            at = slice(r, r + 256)
            value = dot3((phigh[at, :near], plow[at, :near]), (high[lines, :], low[lines, :]))
            value += dot3((phigh[at, near:], plow[at, near:]), (far_high[lines, :], far_low[lines, :]))
            out[at, lines] = value


def lower_blocks(update, left, right):
    at = 0
    for a in range(4):
        value = dot3([v[a * B : (a + 1) * B] for v in left], [v[: (a + 1) * B] for v in right])
        for b in range(a + 1):
            update[at * B : (at + 1) * B, :] = value[:, b * B : (b + 1) * B]
            at += 1


def finish_kernel(child, mine, received, panel, meta, *refs):
    off, update = refs[-2:]
    wide = jnp.concatenate([column_mask(meta, child)] * 4, axis=1)
    masks = wide * meta[child : child + 1, :SW]
    product = (mine[...] + received[...]) * masks
    off[...] = -product
    lower_blocks(update, split(product), split(panel[...] * masks))


def sum_kernel(parts, out):
    total = parts[0]
    for k in range(1, 8):
        total += parts[k]
    for k in range(8):
        out[k] = total


def child_kernel(parts, diag, meta, out):
    at = 0
    for child in range(2):
        across = lax.broadcasted_iota(jnp.int32, (1, SW), 1).astype(F32) < meta[2 + child : 3 + child, :SW]
        across = across.astype(F32)
        mask = column_mask(meta, child)
        for a in range(4):
            for b in range(a + 1):
                block = parts[at]
                at += 1
                for (i, j), value in {(b, a): block.T, (a, b): block}.items():
                    lines = slice(child * SW + i * B, child * SW + (i + 1) * B)
                    lanes = slice(j * B, (j + 1) * B)
                    rows = mask[i * B : (i + 1) * B]
                    out[lines, lanes] = (diag[lines, lanes] + value) * rows * across[:, lanes]


def after(value, *before):
    return lax.optimization_barrier((value, *before))[0]


def local(anc_inverse, panel, diag_inverse, widths, pattern):
    names = ("core", "y", "zl", "zh", "x")
    ids = jnp.stack([lax.axis_index(n) for n in names]).astype(jnp.int32)
    meta = call(meta_kernel, struct((8, WIDE)), [SMEM] * 3)(ids, widths, pattern)
    rounds, table = z_rounds()
    got = [lax.ppermute(anc_inverse, Z, pairs) for pairs in rounds]
    held = jnp.stack(got)

    left, right = step(panel, "y", 1), step(after(panel, got[0]), "y", -1)
    half = SW // 2
    far = [(step(left[a : a + half], "y", 1), step(right[a + half : a + SW], "y", -1)) for a in (0, SW)]

    before, beyond = step(held, "x", 1), step(held, "x", -1)
    near = [after(held, meta), before, beyond]
    near += [step(value, "core", 1, 2) for value in near]
    ends = step(before[:2], "x", 1), step(beyond[2:], "x", -1)
    parts = call(
        functools.partial(near_kernel, table), [struct((SW, 12 * B), BF16)] * 4, [SMEM] + [VMEM] * 6
    )(ids, *near)
    ends = tuple(after(value, parts[0], *far[0]) for value in ends)
    ends += tuple(step(value, "core", 1, 2) for value in ends)

    def product(role, first):
        pair = [struct((SW, SW), BF16)] * 2
        anc = call(functools.partial(far_kernel, table, role), pair, [SMEM] + [VMEM] * 4)(ids, first, *ends[1:])
        anc = (*parts[2 * role : 2 * role + 2], *anc)
        values = []
        for child in range(2):
            block = pl.BlockSpec((SW, SW), lambda g, child=child: (child, 0))
            values.append(
                pl.pallas_call(
                    functools.partial(product_kernel, child),
                    grid=(1,),
                    out_shape=struct((SW, SW)),
                    in_specs=[SMEM] + [block] * 3 + [VMEM] * 7,
                    out_specs=VMEM,
                    scratch_shapes=[pltpu.VMEM((SW, WIDE), BF16)] * 2,
                    compiler_params=pltpu.CompilerParams(vmem_limit_bytes=36 * 2**20),
                    cost_estimate=pl.CostEstimate(flops=1024, bytes_accessed=1024, transcendentals=0),
                )(ids, after(panel, *values) if values else panel, left, right, *far[child], *anc, meta)
            )
        return values

    sent = product(0, ends[0])
    received = [step(value, "zl", 1, 2) for value in sent]
    mine = product(1, after(ends[0], sent[1]))

    off, updates = None, []
    for child in range(2):
        block = pl.BlockSpec((SW, SW), lambda g, child=child: (child, 0))
        off, update = pl.pallas_call(
            functools.partial(finish_kernel, child),
            grid=(1,),
            out_shape=(struct(panel.shape), struct((10 * B, B))),
            in_specs=[VMEM, VMEM, block, VMEM] + [pl.BlockSpec(memory_space=pl.ANY)] * child,
            out_specs=[block, VMEM],
            input_output_aliases={4: 0} if child else {},
            compiler_params=pltpu.CompilerParams(vmem_limit_bytes=LIMIT),
            cost_estimate=pl.CostEstimate(flops=1024, bytes_accessed=1024, transcendentals=0),
        )(mine[child], received[child], panel, meta, *([off] if child else []))
        updates.append(update)

    def swap(value):
        return lax.all_to_all(value, ROW, 0, 0, tiled=True)

    shape = (8, 20 * B // 8, B)
    spread = swap(jnp.concatenate(updates, axis=0).reshape(shape))
    summed = swap(call(sum_kernel, struct(shape), [VMEM])(spread)).reshape(20, B, B)
    out = call(child_kernel, struct(diag_inverse.shape), [VMEM] * 3)(summed, diag_inverse, meta)
    return off, out


def solution(mesh):
    fine = Mesh(mesh.devices.reshape(2, 4, 2, 4, 4), ("core", "y", "zl", "zh", "x"))
    group = ("core", "zh", "x")
    in_specs = (P(ROW, group), P(group, ROW), P(group, None), P(), P())
    out_specs = (P(group, ROW), P(group, None))
    return jax.shard_map(local, mesh=fine, in_specs=in_specs, out_specs=out_specs, check_vma=False)
```

```python
import functools

import jax
import jax.numpy as jnp
from jax import lax
from jax.experimental import pallas as pl
from jax.experimental.pallas import tpu as pltpu
from jax.sharding import Mesh, PartitionSpec as P

B = 128
SW = 512
WIDE = 2048
PACKED = 1056
LIMIT = 22 * 2**20
ROW = ("y", "zl")
Z = ("zl", "zh")
DIRECTIONS = (0, 3, 1, 2)

VMEM = pl.BlockSpec(memory_space=pltpu.VMEM)
SMEM = pl.BlockSpec(memory_space=pltpu.SMEM)
F32 = jnp.float32
BF16 = jnp.bfloat16


def call(kernel, out_shape, specs, out_specs=None, scratch=(), aliases=None):
    single = not isinstance(out_shape, (tuple, list))
    return pl.pallas_call(
        kernel,
        out_shape=out_shape,
        in_specs=specs,
        out_specs=out_specs if out_specs is not None else (VMEM if single else [VMEM] * len(out_shape)),
        scratch_shapes=list(scratch),
        input_output_aliases=aliases or {},
        compiler_params=pltpu.CompilerParams(vmem_limit_bytes=LIMIT),
        cost_estimate=pl.CostEstimate(flops=1024, bytes_accessed=1024, transcendentals=0),
    )


def struct(shape, dtype=F32):
    return jax.ShapeDtypeStruct(shape, dtype)


def z_rounds():
    even = [
        {0: 0, 2: 1, 4: 4, 6: 5},
        {6: 0, 0: 1, 2: 4, 4: 5},
        {2: 0, 4: 1, 6: 4, 0: 5},
        {4: 0, 6: 1, 0: 4, 2: 5},
    ]
    rounds = []
    table = {}
    for k, pairs in enumerate(even):
        pairs = {**pairs, **{(3 - t) % 8: (3 - s) % 8 for t, s in pairs.items()}}
        rounds.append([((s % 2) * 4 + s // 2, (t % 2) * 4 + t // 2) for t, s in pairs.items()])
        for t, s in pairs.items():
            table[t, int(s % 2 == t % 2), (s // 2) // 2] = k
    return rounds, table


def step(value, axis, k, n=4):
    return lax.ppermute(value, axis, [(i, (i + k) % n) for i in range(n)])


def split(value):
    high = value.astype(BF16)
    return high, (value - high.astype(F32)).astype(BF16)


def dot3(a, b):
    dims = (((1,), (1,)), ((), ()))
    mul = functools.partial(lax.dot_general, dimension_numbers=dims, preferred_element_type=F32)
    return mul(a[0], b[0]) + (mul(a[0], b[1]) + mul(a[1], b[0]))


def meta_kernel(ids, widths, pattern, out):
    core, y, zl, zh, x = (ids[i] for i in range(5))
    first = ((core * 4 + zh) * 4 + x) * 2
    for child in range(2):
        for d, shift in enumerate(DIRECTIONS):
            block = ((y + shift) % 4 * 2 + zl) * 4
            for k in range(4):
                value = pattern[first + child, block + k].astype(F32)
                out[child : child + 1, (d * 4 + k) * B : (d * 4 + k + 1) * B] = jnp.full((1, B), value)
        out[2 + child : 3 + child, :] = jnp.full((1, WIDE), (widths[first + child] * B).astype(F32))
    out[4:8, :] = jnp.zeros((4, WIDE), F32)


def column_mask(meta, child):
    position = lax.broadcasted_iota(jnp.int32, (SW, B), 0).astype(F32)
    return (position < meta[2 + child : 3 + child, :B]).astype(F32)


def place_of(table, ids, role, half):
    z = ids[3] * 2 + ids[2]
    places = [jnp.int32(0)] * 2
    for k in range(2):
        for at in range(8):
            places[k] = jnp.where(z == at, table[at, role, k], places[k])
    return jnp.where(half == 0, *places)


def each_block(table, ids, role, body):
    @pl.loop(0, 4)
    def _(d):
        block = (ids[1] + jnp.where(d == 0, 0, jnp.where(d == 1, 3, jnp.where(d == 2, 1, 2)))) % 4
        body(d, block // 2 == ids[0], place_of(table, ids, role, block % 2))


def near_kernel(table, ids, *refs):
    for role in range(2):
        high, low = refs[6 + 2 * role : 8 + 2 * role]

        def body(d, here, place):
            for a in range(3):
                lanes = pl.ds(pl.multiple_of((a * 4 + d) * B, B), B)
                for when, ref in ((here, refs[a]), (jnp.logical_not(here), refs[3 + a])):

                    @pl.when(when)
                    def _():
                        high[:, lanes], low[:, lanes] = split(ref[place])

        each_block(table, ids, role, body)


def far_kernel(table, role, ids, *refs):
    high, low = refs[4:]

    def body(d, here, place):
        lanes = pl.ds(pl.multiple_of(d * B, B), B)
        for core, when in ((0, here), (1, jnp.logical_not(here))):
            for side, where in ((0, place < 2), (1, place >= 2)):

                @pl.when(when & where)
                def _():
                    high[:, lanes], low[:, lanes] = split(refs[2 * core + side][place % 2])

    each_block(table, ids, role, body)


def product_kernel(child, ids, own, left, right, top, bottom, *refs):
    high, low, far_high, far_low, meta, out, phigh, plow = refs
    mask = column_mask(meta, child)
    for a, away in enumerate((0, 3, 1, 2)):
        k = (ids[4] + away) % 4
        for d, source in enumerate((own, left, right, None)):
            here = pl.ds(pl.multiple_of(k * B, B), B)
            across = pl.ds(pl.multiple_of((d * 4 + k) * B, B), B)
            lanes = slice((a * 4 + d) * B, (a * 4 + d + 1) * B)
            if source is None:
                value = jnp.concatenate([top[:, here], bottom[:, here]], axis=0)
            else:
                value = source[:, here]
            phigh[:, lanes], plow[:, lanes] = split(value * mask * meta[child : child + 1, across])
    near = 12 * B
    for n in range(0, SW, 256):
        lines = slice(n, n + 256)
        for r in range(0, SW, 256):
            at = slice(r, r + 256)
            value = dot3((phigh[at, :near], plow[at, :near]), (high[lines, :], low[lines, :]))
            value += dot3((phigh[at, near:], plow[at, near:]), (far_high[lines, :], far_low[lines, :]))
            out[at, lines] = value


def lower_blocks(update, pairs):
    at = 0
    diagonal = []
    for a in range(4):
        value = None
        for left, right in pairs:
            term = dot3([v[a * B : (a + 1) * B] for v in left], [v[: (a + 1) * B] for v in right])
            value = term if value is None else value + term
        for b in range(a):
            update[at * B : (at + 1) * B, :] = value[:, b * B : (b + 1) * B]
            at += 1
        diagonal.append(value[:, a * B :])
    line, lane = (lax.broadcasted_iota(jnp.int32, (B, B), axis) for axis in range(2))
    update[8 * B :, :] = jnp.zeros((PACKED - 8 * B, B), F32)
    for k in range(2):
        first, second = diagonal[2 * k : 2 * k + 2]
        update[at * B : (at + 1) * B, :] = jnp.where(line >= lane, first, second)
        update[8 * B + k : 8 * B + k + 1, :] = jnp.sum(jnp.where(line == lane, second, 0.0), axis=0, keepdims=True)
        at += 1


def finish_kernel(child, mine, received, panel, meta, *refs):
    off, update = refs[-2:]
    wide = jnp.concatenate([column_mask(meta, child)] * 4, axis=1)
    masks = wide * meta[child : child + 1, :SW]
    product = (mine[...] + received[...]) * masks
    off[...] = -product
    lower_blocks(update, [(split(product), split(panel[...] * masks))])


def sum_kernel(parts, out):
    total = parts[0]
    for k in range(1, 8):
        total += parts[k]
    for k in range(8):
        out[k] = total


def child_kernel(parts, diag, meta, out):
    line, lane = (lax.broadcasted_iota(jnp.int32, (B, B), axis) for axis in range(2))
    for child in range(2):
        base = child * PACKED
        across = lax.broadcasted_iota(jnp.int32, (1, SW), 1).astype(F32) < meta[2 + child : 3 + child, :SW]
        across = across.astype(F32)
        mask = column_mask(meta, child)

        def put(i, j, value):
            lines = slice(child * SW + i * B, child * SW + (i + 1) * B)
            lanes = slice(j * B, (j + 1) * B)
            out[lines, lanes] = (diag[lines, lanes] + value) * mask[i * B : (i + 1) * B] * across[:, lanes]

        at = base
        for a in range(4):
            for b in range(a):
                block = parts[at : at + B, :]
                put(a, b, block)
                put(b, a, block.T)
                at += B
        for k in range(2):
            block = parts[at : at + B, :]
            turned = block.T
            row = parts[base + 8 * B + k : base + 8 * B + k + 1, :]
            put(2 * k, 2 * k, jnp.where(line >= lane, block, turned))
            put(2 * k + 1, 2 * k + 1, jnp.where(line < lane, block, jnp.where(line > lane, turned, row)))
            at += B


def after(value, *before):
    return lax.optimization_barrier((value, *before))[0]


def local(anc_inverse, panel, diag_inverse, widths, pattern):
    names = ("core", "y", "zl", "zh", "x")
    ids = jnp.stack([lax.axis_index(n) for n in names]).astype(jnp.int32)
    meta = call(meta_kernel, struct((8, WIDE)), [SMEM] * 3)(ids, widths, pattern)
    rounds, table = z_rounds()
    got = [lax.ppermute(anc_inverse, Z, pairs) for pairs in rounds]
    held = jnp.stack(got)

    left, right = step(panel, "y", 1), step(after(panel, got[0]), "y", -1)
    half = SW // 2
    far = [(step(left[a : a + half], "y", 1), step(right[a + half : a + SW], "y", -1)) for a in (0, SW)]

    before, beyond = step(held, "x", 1), step(held, "x", -1)
    near = [after(held, meta), before, beyond]
    near += [step(value, "core", 1, 2) for value in near]
    ends = step(before[:2], "x", 1), step(beyond[2:], "x", -1)
    parts = call(
        functools.partial(near_kernel, table), [struct((SW, 12 * B), BF16)] * 4, [SMEM] + [VMEM] * 6
    )(ids, *near)
    ends = tuple(after(value, parts[0], *far[0]) for value in ends)
    ends += tuple(step(value, "core", 1, 2) for value in ends)

    def product(role, first):
        pair = [struct((SW, SW), BF16)] * 2
        anc = call(functools.partial(far_kernel, table, role), pair, [SMEM] + [VMEM] * 4)(ids, first, *ends[1:])
        anc = (*parts[2 * role : 2 * role + 2], *anc)
        values = []
        for child in range(2):
            block = pl.BlockSpec((SW, SW), lambda g, child=child: (child, 0))
            values.append(
                pl.pallas_call(
                    functools.partial(product_kernel, child),
                    grid=(1,),
                    out_shape=struct((SW, SW)),
                    in_specs=[SMEM] + [block] * 3 + [VMEM] * 7,
                    out_specs=VMEM,
                    scratch_shapes=[pltpu.VMEM((SW, WIDE), BF16)] * 2,
                    compiler_params=pltpu.CompilerParams(vmem_limit_bytes=36 * 2**20),
                    cost_estimate=pl.CostEstimate(flops=1024, bytes_accessed=1024, transcendentals=0),
                )(ids, after(panel, *values) if values else panel, left, right, *far[child], *anc, meta)
            )
        return values

    sent = product(0, ends[0])
    received = [step(value, "zl", 1, 2) for value in sent]
    mine = product(1, after(ends[0], sent[1]))

    off, updates = None, []
    for child in range(2):
        block = pl.BlockSpec((SW, SW), lambda g, child=child: (child, 0))
        off, update = pl.pallas_call(
            functools.partial(finish_kernel, child),
            grid=(1,),
            out_shape=(struct(panel.shape), struct((PACKED, B))),
            in_specs=[VMEM, VMEM, block, VMEM] + [pl.BlockSpec(memory_space=pl.ANY)] * child,
            out_specs=[block, VMEM],
            input_output_aliases={4: 0} if child else {},
            compiler_params=pltpu.CompilerParams(vmem_limit_bytes=LIMIT),
            cost_estimate=pl.CostEstimate(flops=1024, bytes_accessed=1024, transcendentals=0),
        )(mine[child], received[child], panel, meta, *([off] if child else []))
        updates.append(update)

    def swap(value):
        return lax.all_to_all(value, ROW, 0, 0, tiled=True)

    shape = (8, 2 * PACKED // 8, B)
    spread = swap(jnp.concatenate(updates, axis=0).reshape(shape))
    summed = swap(call(sum_kernel, struct(shape), [VMEM])(spread)).reshape(2 * PACKED, B)
    out = call(child_kernel, struct(diag_inverse.shape), [VMEM] * 3)(summed, diag_inverse, meta)
    return off, out


def solution(mesh):
    fine = Mesh(mesh.devices.reshape(2, 4, 2, 4, 4), ("core", "y", "zl", "zh", "x"))
    group = ("core", "zh", "x")
    in_specs = (P(ROW, group), P(group, ROW), P(group, None), P(), P())
    out_specs = (P(group, ROW), P(group, None))
    return jax.shard_map(local, mesh=fine, in_specs=in_specs, out_specs=out_specs, check_vma=False)
```
